32 devices in a mesh: dp: 16 (over z, y, x), shard: 2 (over core).
Axes of the slice: x: 2, y: 2, z: 4, core: 2. Of those that a mesh axis runs over, the one named last changes fastest.
Arguments:
- features: bfloat16 [65536, 100], P(('dp', 'shard')), may hold values from -6 to 6
- neighbors: int32 [65536, 8], P(('dp', 'shard')), may hold values from 0 to 1023
- label_mask: int32 [65536], P(('dp', 'shard')), may hold values from 0 to 1
- labels: int32 [65536], P(('dp', 'shard')), may hold values from 0 to 46
- w_first: float32 [100, 2048], P(None, ('dp', 'shard')), may hold values from -0.625 to 0.625
- w_second: float32 [2048, 47], P(('dp', 'shard')), may hold values from -0.125 to 0.125
- b_first: float32 [2048], P(('dp', 'shard')), may hold values from -0.6 to 0.6
- b_second: float32 [47], replicated, may hold values from -1.8 to 1.8
- l_first: float32 [100, 100], replicated
- r_first: float32 [2048, 2048], P(None, ('dp', 'shard'))
- l_second: float32 [2048, 2048], P(('dp', 'shard'))
- r_second: float32 [47, 47], replicated
- l_first_root: float32 [100, 100], replicated
- r_first_root: float32 [2048, 2048], P(None, ('dp', 'shard'))
- l_second_root: float32 [2048, 2048], P(('dp', 'shard'))
- r_second_root: float32 [47, 47], replicated
- m_first: float32 [2048], P(('dp', 'shard'))
- v_first: float32 [2048], P(('dp', 'shard')), as said below
- m_second: float32 [47], replicated
- v_second: float32 [47], replicated, as said below
Outputs:
- loss_sum: float32 [], replicated
- label_count: float32 [], replicated
- clip_norm: float32 [], replicated
- grad_first: float32 [100, 2048], P(None, ('dp', 'shard'))
- grad_second: float32 [2048, 47], P(('dp', 'shard'))
- new_w_first: float32 [100, 2048], P(None, ('dp', 'shard'))
- new_w_second: float32 [2048, 47], P(('dp', 'shard'))
- new_l_first: float32 [100, 100], replicated
- new_r_first: float32 [2048, 2048], P(None, ('dp', 'shard'))
- new_l_second: float32 [2048, 2048], P(('dp', 'shard'))
- new_r_second: float32 [47, 47], replicated
- new_m_first: float32 [2048], P(('dp', 'shard'))
- new_v_first: float32 [2048], P(('dp', 'shard'))
- new_b_first: float32 [2048], P(('dp', 'shard'))
- new_m_second: float32 [47], replicated
- new_v_second: float32 [47], replicated
- new_b_second: float32 [47], replicated
The draws below stay inside these ranges and needn't reach their ends.
Inputs may be any that keep to these rules, and one draw needn't show every extreme that they name: `neighbors`: each entry is a row within the node's own block of 1024 consecutive rows. `v_first`: positive. `v_second`: positive.
All inputs are finite; a program needn't handle non-finite values.
Results may differ from the reference program's by a relative error of at most 0.0057.
Values may be sent and summed in bfloat16 or wider, within the bound.
No kernel may reach another device: no remote copies, remote signals or barrier semaphores. Data moves between devices by JAX's collectives and lax.ppermute only.
A program may use at most 128 MiB of HBM per device.

```python
import math
import jax
import jax.numpy as jnp
from jax import lax

F_IN = 100
HID = 2048
CLASSES = 47
NB = 1024
MB = 2
DEG = 8
STEP = 10
NODES = 65536
N_DP = 16
N_SHARD = 2


clip_limit = 0.05


beta_stat = 0.95


beta_one = 0.9


beta_two = 0.999


def entry_level():
    return clip_limit / math.sqrt(F_IN * HID + HID * CLASSES)


def square_draw(key, order, level, spread_lo, spread_hi):
    key_diag, key_off = jax.random.split(key)
    factor = jnp.exp(jax.random.uniform(key_diag, (order,), jnp.float32, math.log(spread_lo), math.log(spread_hi)))
    noise = jax.random.normal(key_off, (order, order), jnp.float32) * (0.3 / math.sqrt(order))
    diag_mask = jnp.eye(order, dtype=jnp.float32)
    return level * (diag_mask * factor[None, :] + noise * (1.0 - diag_mask))


def stat_level(length):
    return (1.0 - beta_stat) / beta_stat * length * entry_level() ** 2


def first_square():
    return clip_limit ** 2 * 270.0 * F_IN / (NODES * HID)


def first_stat_level(order):
    return 0.0224 * first_square() / math.sqrt(order)


def draw_label_mask(key, part):
    key = jax.random.fold_in(key, 11)
    rows_all = jnp.arange(NODES, dtype=jnp.int32)
    device = rows_all // (MB * NB)
    outer = device // N_SHARD
    inner = device % N_SHARD
    thresh = (N_DP - 1 + 2 * outer) * (N_SHARD - 1 + 2 * inner) * 100 // ((N_DP - 1) * (N_SHARD - 1))
    picks = jax.random.randint(key, (NODES,), 0, 1000)
    return (picks < thresh).astype(jnp.int32)


def draw_l_first(key, part):
    key = jax.random.fold_in(key, 21)
    return square_draw(key, F_IN, first_stat_level(F_IN), 1.0, 4.0)


def draw_r_first(key, part):
    key = jax.random.fold_in(key, 22)
    return square_draw(key, HID, first_stat_level(HID), 1.0, 4.0)


def draw_l_second(key, part):
    key = jax.random.fold_in(key, 23)
    return square_draw(key, HID, stat_level(CLASSES), 1.0, 4.0)


def draw_r_second(key, part):
    key = jax.random.fold_in(key, 24)
    return square_draw(key, CLASSES, stat_level(HID), 1.0, 4.0)


def draw_l_first_root(key, part):
    key = jax.random.fold_in(key, 31)
    return square_draw(key, F_IN, 1.0, 0.5, 2.0)


def draw_r_first_root(key, part):
    key = jax.random.fold_in(key, 32)
    return square_draw(key, HID, 1.0, 0.5, 2.0)


def draw_l_second_root(key, part):
    key = jax.random.fold_in(key, 33)
    return square_draw(key, HID, 1.0, 0.5, 2.0)


def draw_r_second_root(key, part):
    key = jax.random.fold_in(key, 34)
    return square_draw(key, CLASSES, 1.0, 0.5, 2.0)


def first_moment(key, length):
    level = (1.0 - beta_one) / beta_one * 4.0 * entry_level()
    return jax.random.normal(key, (length,), jnp.float32) * level


def second_moment(key, length):
    level = (1.0 - beta_two) / beta_two * (4.0 * entry_level()) ** 2
    return level * jnp.exp(jax.random.uniform(key, (length,), jnp.float32, 0.0, math.log(4.0)))


def draw_m_first(key, part):
    key = jax.random.fold_in(key, 41)
    return first_moment(key, HID)


def draw_v_first(key, part):
    key = jax.random.fold_in(key, 42)
    return second_moment(key, HID)


def draw_m_second(key, part):
    key = jax.random.fold_in(key, 43)
    return first_moment(key, CLASSES)


def draw_v_second(key, part):
    key = jax.random.fold_in(key, 44)
    return second_moment(key, CLASSES)


def plant(entries, stream_key, smallest, largest):
    longest = entries.shape.index(max(entries.shape))
    spots = []
    for shift in (0, 1):
        where = [jax.random.randint(jax.random.fold_in(stream_key, axis), (), 0, length) for axis, length in enumerate(entries.shape)]
        where[longest] = (where[longest] + shift) % entries.shape[longest]
        spots.append(tuple(where))
    return entries.at[spots[0]].set(smallest).at[spots[1]].set(largest)


def block_levels(rng, extent, cuts, smallest, largest):
    factor_of, own = 1.0, jax.random.fold_in(rng, 6)
    for axis_at, shards_of in cuts:
        steps = jnp.exp(jax.random.uniform(jax.random.fold_in(own, axis_at), (shards_of,), jnp.float32, smallest / len(cuts), largest / len(cuts)))
        factor_of = factor_of * jnp.repeat(steps, extent[axis_at] // shards_of).reshape([-1 if axis == axis_at else 1 for axis in range(len(extent))])
    return factor_of


def scatter_about(own_key, dims, deviation, bound, cuts=(), held_as=jnp.bfloat16):
    values = deviation * jax.random.normal(own_key, dims, jnp.float32)
    if cuts:
        values = values * block_levels(own_key, dims, cuts, -0.22, 0.18)
    return jnp.clip(values, -bound, bound).astype(held_as)


def setup_inputs(seed: int = 0) -> dict:
    splits = jax.random.split(jax.random.key(seed), 21)
    features = scatter_about(splits[0], (NODES, F_IN), 1.0, 6.0, ((0, 32),))
    neighbors = plant(jax.random.randint(splits[1], (NODES, DEG), 0, NB), jax.random.fold_in(splits[1], 1), 0, NB - 1).astype(jnp.int32)
    label_mask = draw_label_mask(jax.random.fold_in(splits[20], 71), 0)
    labels = plant(jax.random.randint(splits[3], (NODES,), 0, CLASSES), jax.random.fold_in(splits[3], 1), 0, CLASSES - 1).astype(jnp.int32)
    w_first = scatter_about(splits[4], (F_IN, HID), F_IN ** -0.5, 0.625, ((1, 32),), jnp.float32)
    w_second = scatter_about(splits[5], (HID, CLASSES), HID ** -0.5, 0.125, ((0, 32),), jnp.float32)
    b_first = scatter_about(splits[6], (HID,), 0.1, 0.6, ((0, 32),), jnp.float32)
    b_second = scatter_about(splits[7], (CLASSES,), 0.3, 1.8, (), jnp.float32)
    l_first = draw_l_first(jax.random.fold_in(splits[20], 71), 0)
    r_first = draw_r_first(jax.random.fold_in(splits[20], 71), 0)
    l_second = draw_l_second(jax.random.fold_in(splits[20], 71), 0)
    r_second = draw_r_second(jax.random.fold_in(splits[20], 71), 0)
    l_first_root = draw_l_first_root(jax.random.fold_in(splits[20], 71), 0)
    r_first_root = draw_r_first_root(jax.random.fold_in(splits[20], 71), 0)
    l_second_root = draw_l_second_root(jax.random.fold_in(splits[20], 71), 0)
    r_second_root = draw_r_second_root(jax.random.fold_in(splits[20], 71), 0)
    m_first = draw_m_first(jax.random.fold_in(splits[20], 71), 0)
    v_first = draw_v_first(jax.random.fold_in(splits[20], 71), 0)
    m_second = draw_m_second(jax.random.fold_in(splits[20], 71), 0)
    v_second = draw_v_second(jax.random.fold_in(splits[20], 71), 0)
    return dict(features=features, neighbors=neighbors, label_mask=label_mask, labels=labels, w_first=w_first, w_second=w_second, b_first=b_first, b_second=b_second, l_first=l_first, r_first=r_first, l_second=l_second, r_second=r_second, l_first_root=l_first_root, r_first_root=r_first_root, l_second_root=l_second_root, r_second_root=r_second_root, m_first=m_first, v_first=v_first, m_second=m_second, v_second=v_second)


clip_limit = 0.05
beta_stat = 0.95
beta_one = 0.9
beta_two = 0.999
adam_eps = 1e-08
decay_rate = 0.01
rate_bias = 0.2
rate_first = 1000.0
rate_second = 300.0
highest = lax.Precision.HIGHEST

@jax.custom_vjp
def low(v):
    return lax.optimization_barrier(v.astype(jnp.bfloat16)).astype(jnp.float32)

@jax.custom_vjp
def low_back(v):
    return v

def low_keep(v):
    return (low(v), None)

def low_pass(kept, grad):
    return (grad,)

def back_keep(v):
    return (v, None)

def back_low(kept, grad):
    return (low(grad),)
low.defvjp(low_keep, low_pass)
low_back.defvjp(back_keep, back_low)

def adjacency(neighbors):
    node_count = neighbors.shape[0]
    columns = jnp.arange(node_count, dtype=jnp.int32)
    counts = lax.optimization_barrier(jnp.sum((neighbors[:, :, None] == columns[None, None, :]).astype(jnp.float32), axis=1))
    identity = jnp.eye(node_count, dtype=jnp.float32)
    self_count = lax.optimization_barrier(jnp.sum(counts * identity, axis=1))
    return counts + identity * (2.0 + self_count)[:, None]

def forward_block(inputs, params):
    feature_rows, neighbor_rows, mask_rows, label_rows = inputs
    first_q, second_q, bias_q, bias_two = params
    matrix = adjacency(neighbor_rows)
    scale_in = 1.0 / (neighbor_rows.shape[1] + 1)
    pooled_one = low(jnp.dot(matrix, feature_rows, precision=highest) * scale_in)
    hidden_pre = low_back(jnp.dot(pooled_one, first_q, precision=highest) + bias_q)
    hidden = low(jax.nn.gelu(hidden_pre))
    pooled_two = low_back(low(jnp.dot(matrix, hidden, precision=highest) * scale_in))
    logits = low_back(jnp.dot(pooled_two, second_q, precision=highest) + bias_two)
    log_prob = jax.nn.log_softmax(logits, axis=-1)
    onehot = (label_rows[:, None] == jnp.arange(logits.shape[1], dtype=jnp.int32)[None, :]).astype(jnp.float32)
    losses = -lax.optimization_barrier(jnp.sum(log_prob * onehot, axis=-1))
    return jnp.sum(losses * mask_rows.astype(jnp.float32))

def adam_step(param, grad, first, second):
    first_new = beta_one * first + (1.0 - beta_one) * grad
    second_new = beta_two * second + (1.0 - beta_two) * grad * grad
    corr_one = 1.0 - beta_one ** STEP
    corr_two = 1.0 - beta_two ** STEP
    update = first_new / corr_one / (jnp.sqrt(second_new / corr_two) + adam_eps) + decay_rate * param
    return (first_new, second_new, param - rate_bias * update)

def reference(features, neighbors, label_mask, labels, w_first, w_second, b_first, b_second, l_first, r_first, l_second, r_second, l_first_root, r_first_root, l_second_root, r_second_root, m_first, v_first, m_second, v_second):
    blocks = features.shape[0] // NB
    feature_blocks = features.astype(jnp.float32).reshape(blocks, NB, F_IN)
    neighbor_blocks = neighbors.reshape(blocks, NB, DEG)
    mask_blocks = label_mask.reshape(blocks, NB)
    label_blocks = labels.reshape(blocks, NB)
    label_count = jnp.sum(label_mask).astype(jnp.float32)
    denom = jnp.maximum(label_count, 1.0)

    def objective(first_w, second_w, first_b, second_b):
        params = (low(first_w), low(second_w), low(first_b), second_b)
        block_fn = jax.checkpoint(lambda inputs: forward_block(inputs, params))
        block_sums = lax.map(block_fn, (feature_blocks, neighbor_blocks, mask_blocks, label_blocks))
        loss_total = jnp.sum(block_sums)
        return (loss_total / denom, loss_total)
    scaled, grad_fn, loss_sum = jax.vjp(objective, w_first, w_second, b_first, b_second, has_aux=True)
    g_first, g_second, gb_first, gb_second = grad_fn(jnp.ones_like(scaled))
    squares = jnp.sum(g_first * g_first) + jnp.sum(g_second * g_second) + jnp.sum(gb_first * gb_first) + jnp.sum(gb_second * gb_second)
    clip_norm = jnp.sqrt(squares)
    factor = jnp.minimum(1.0, clip_limit / (clip_norm + 1e-06))
    grad_first = g_first * factor
    grad_second = g_second * factor
    new_l_first = beta_stat * l_first + (1.0 - beta_stat) * jnp.dot(grad_first, grad_first.T, precision=highest)
    new_r_first = beta_stat * r_first + (1.0 - beta_stat) * jnp.dot(grad_first.T, grad_first, precision=highest)
    new_w_first = w_first - rate_first * jnp.dot(jnp.dot(l_first_root, grad_first, precision=highest), r_first_root, precision=highest)
    new_l_second = beta_stat * l_second + (1.0 - beta_stat) * jnp.dot(grad_second, grad_second.T, precision=highest)
    new_r_second = beta_stat * r_second + (1.0 - beta_stat) * jnp.dot(grad_second.T, grad_second, precision=highest)
    new_w_second = w_second - rate_second * jnp.dot(jnp.dot(l_second_root, grad_second, precision=highest), r_second_root, precision=highest)
    new_m_first, new_v_first, new_b_first = adam_step(b_first, gb_first * factor, m_first, v_first)
    new_m_second, new_v_second, new_b_second = adam_step(b_second, gb_second * factor, m_second, v_second)
    return (loss_sum, label_count, clip_norm, grad_first, grad_second, new_w_first, new_w_second, new_l_first, new_r_first, new_l_second, new_r_second, new_m_first, new_v_first, new_b_first, new_m_second, new_v_second, new_b_second)
```

```python
import functools

import jax
import jax.numpy as jnp
from jax import lax
from jax.experimental import pallas as pl
from jax.experimental.pallas import tpu as pltpu
from jax.sharding import PartitionSpec as P

STEP = 10
BLOCK = 1024
AXES = ("dp", "shard")

clip_limit = 0.05
beta_stat = 0.95
beta_one = 0.9
beta_two = 0.999
adam_eps = 1e-08
decay_rate = 0.01
rate_bias = 0.2
rate_first = 1000.0
rate_second = 300.0
highest = lax.Precision.HIGHEST

f32 = jnp.float32
bf16 = jnp.bfloat16
NN = (((1,), (0,)), ((), ()))
NT = (((1,), (1,)), ((), ()))
TN = (((0,), (0,)), ((), ()))

ROWS = 160
HALF = 80
TOP = 112
LANES = 128


def mm(a, b, dims=NN):
    return lax.dot_general(a, b, dims, preferred_element_type=f32)


def params(limit=56):
    return pltpu.CompilerParams(vmem_limit_bytes=limit * 2**20)


def cost(us):
    return pl.CostEstimate(flops=int(us * 1e9), bytes_accessed=int(us * 2e6), transcendentals=0)


def adam_step(param, grad, first, second):
    first_new = beta_one * first + (1.0 - beta_one) * grad
    second_new = beta_two * second + (1.0 - beta_two) * grad * grad
    corr_one = 1.0 - beta_one**STEP
    corr_two = 1.0 - beta_two**STEP
    update = (
        first_new / corr_one / (jnp.sqrt(second_new / corr_two) + adam_eps) + decay_rate * param
    )
    return (first_new, second_new, param - rate_bias * update)


def pack_kernel(w1t_ref, w2t_ref, b_ref, out_ref, bottom):
    fan_in = w1t_ref.shape[1]
    width = w1t_ref.shape[0]
    classes = w2t_ref.shape[0]
    rows = lax.broadcasted_iota(jnp.int32, (TOP, fan_in), 0)
    cols = lax.broadcasted_iota(jnp.int32, (TOP, fan_in), 1)
    eye = (rows == cols).astype(bf16)
    w1 = mm(eye, w1t_ref[...].astype(bf16), NT)
    rows = lax.broadcasted_iota(jnp.int32, (TOP, width), 0)
    w1 = jnp.where(rows == fan_in, b_ref[...], w1)
    out_ref[:, 0:width] = w1[0:HALF].astype(bf16)
    bottom[...] = jnp.zeros_like(bottom)
    bottom[0 : TOP - HALF, :] = w1[HALF:TOP]
    bottom[TOP - HALF : TOP - HALF + classes, :] = w2t_ref[...]
    out_ref[:, width : 2 * width] = bottom[...].astype(bf16)


def graph_kernel(fan_in, nbr_ref, feat_ref, m_ref, p_ref, pt_ref):
    classes = nbr_ref.shape[0]
    scale_in = 1.0 / (classes + 1)
    base = lax.broadcasted_iota(jnp.int32, (16, LANES), 0).astype(jnp.int16)
    one = jnp.ones((16, LANES), bf16)
    zero = jnp.zeros((16, LANES), bf16)
    row = lax.broadcasted_iota(jnp.int32, (LANES, LANES), 0)
    col = lax.broadcasted_iota(jnp.int32, (LANES, LANES), 1)
    for t in range(BLOCK // LANES):
        at = slice(t * LANES, (t + 1) * LANES)
        slots = [
            jnp.broadcast_to(nbr_ref[k : k + 1, at], (16, LANES)).astype(jnp.int16)
            for k in range(classes)
        ]
        for u in range(BLOCK // 16):
            here = base + jnp.int16(u * 16)
            terms = [jnp.where(s == here, one, zero) for s in slots]
            while len(terms) > 1:
                terms = [sum(terms[a : a + 2][1:], terms[a]) for a in range(0, len(terms), 2)]
            m_ref[u * 16 : (u + 1) * 16, at] = terms[0]
        square = m_ref[at, at].astype(f32)
        m_ref[at, at] = jnp.where(row == col, 2.0 * square + 2.0, square).astype(bf16)
    pooled = mm(feat_ref[...], m_ref[...]) * scale_in
    rest = LANES - fan_in - 1
    pooled = jnp.concatenate(
        [pooled, jnp.ones((1, BLOCK), f32), jnp.zeros((rest, BLOCK), f32)], axis=0
    )
    pt_ref[...] = pooled[0:TOP].astype(bf16)
    p_ref[...] = pooled.T.astype(bf16)


def main_kernel(nblk, classes, degree, *refs):
    own = refs[0:4]
    other = refs[4:8]
    m_hbm = refs[8 : 8 + nblk]
    p_refs = refs[8 + nblk : 8 + 2 * nblk]
    pt_refs = refs[8 + 2 * nblk : 8 + 3 * nblk]
    mask_ref, label_ref, b2_ref = refs[8 + 3 * nblk : 11 + 3 * nblk]
    keep_ref, send_ref = refs[11 + 3 * nblk : 13 + 3 * nblk]
    w, ww, hid, der, m, z, qq, qqt, row_scr, sem = refs[13 + 3 * nblk :]
    hidden = w.shape[1]
    core = lax.axis_index("shard")
    first = core == 0
    scale_in = 1.0 / (degree + 1)
    copies = [
        pltpu.make_async_copy(m_hbm[b], m.at[b], sem.at[b]) for b in range(nblk)
    ]
    for c in copies:
        c.start()

    lane = lax.broadcasted_iota(jnp.int32, (HALF, LANES), 1)
    left = lane < LANES // 2
    for g in range(4):
        for s in range(4):
            at = slice(s * LANES, (s + 1) * LANES)
            to = slice((g * 4 + s) * LANES, (g * 4 + s + 1) * LANES)
            mine = own[g][:, at].astype(f32)
            theirs = other[g][:, at].astype(f32)
            lo = jnp.where(first, mine, theirs)
            hi = jnp.where(first, theirs, mine)
            w[0:HALF, to] = jnp.where(left, lo, pltpu.roll(hi, LANES // 2, 1)).astype(bf16)
            w[HALF:ROWS, to] = jnp.where(left, pltpu.roll(lo, LANES // 2, 1), hi).astype(bf16)
    ww[0:48, :] = w[TOP:ROWS, :]
    ww[48:96, :] = w[TOP:ROWS, :]
    ww[96:128, :] = jnp.zeros((32, hidden), bf16)

    c0 = 0.7978845608028654
    c1 = c0 * 0.044715
    chunk = 512
    sub = 256
    rows = 256

    def forward(n, _):
        n0 = pl.multiple_of(n * chunk, chunk)
        for b in range(nblk):
            for r in range(BLOCK // rows):
                total = None
                for k in range(chunk // sub):
                    at = pl.ds(n0 + k * sub, sub)
                    to = slice(b * BLOCK + r * rows, b * BLOCK + (r + 1) * rows)
                    x = mm(p_refs[b][r * rows : (r + 1) * rows, :], w[0:LANES, at])
                    x2 = x * x
                    t = jnp.tanh(x * (c0 + c1 * x2))
                    p = 0.5 * t + 0.5
                    h = x * p
                    d = p + h * (1.0 - p) * (2.0 * c0 + 6.0 * c1 * x2)
                    hb = h.astype(bf16)
                    hid[to, at] = hb
                    der[to, at] = d.astype(bf16)
                    part = mm(hb, w[TOP:ROWS, at], NT)
                    total = part if total is None else total + part
                z[to, 0:48] += total
        return 0

    z[...] = jnp.zeros_like(z)
    lax.fori_loop(0, hidden // chunk, forward, 0)

    row_scr[...] = jnp.zeros_like(row_scr)
    loss = jnp.zeros((1, 1), f32)
    count = jnp.zeros((1, 1), f32)
    for b in range(nblk):
        copies[b].wait()
        zb = z[b * BLOCK : (b + 1) * BLOCK, :].T
        zb = zb[0:48]
        z_hi = zb.astype(bf16)
        z_lo = (zb - z_hi.astype(f32)).astype(bf16)
        both = mm(jnp.concatenate([z_hi, z_lo], axis=0), m[b])
        logits = (both[0:48] + both[48:96]) * scale_in + b2_ref[...]
        cls = lax.broadcasted_iota(jnp.int32, (48, BLOCK), 0)
        logits = jnp.where(cls < classes, logits, -1e30)
        top = jnp.max(logits, axis=0, keepdims=True)
        e = jnp.exp(logits - top)
        total = jnp.sum(e, axis=0, keepdims=True)
        hit = cls == label_ref[b : b + 1, :]
        weight = mask_ref[b : b + 1, :].astype(f32)
        picked = jnp.sum(jnp.where(hit, logits, 0.0), axis=0, keepdims=True)
        loss += jnp.sum((jnp.log(total) + top - picked) * weight, axis=1, keepdims=True)
        count += jnp.sum(weight, axis=1, keepdims=True)
        grad = ((e / total - hit.astype(f32)) * weight).astype(bf16)
        row_scr[:, 0:48] += mm(jnp.ones((8, BLOCK), bf16), grad, NT)
        q = mm(grad, m[b], NT) * scale_in
        q_hi = q.astype(bf16)
        q_lo = q - q_hi.astype(f32)
        q2 = jnp.concatenate([q_hi.astype(f32), q_lo, jnp.zeros((32, BLOCK), f32)], axis=0)
        qqt[b] = q2[0:96].astype(bf16)
        qq[b * BLOCK : (b + 1) * BLOCK, :] = q2.T.astype(bf16)

    vec = row_scr[0:1, :]
    pos = lax.broadcasted_iota(jnp.int32, vec.shape, 1)
    vec = jnp.where(pos == 48, loss, jnp.where(pos == 49, count, vec))
    part_a = vec.astype(bf16).astype(f32)
    part_b = (vec - part_a).astype(bf16).astype(f32)
    part_c = (vec - part_a - part_b).astype(bf16).astype(f32)
    r16 = lax.broadcasted_iota(jnp.int32, (16, vec.shape[1]), 0) - jnp.where(first, 5, 8)
    scal = (
        jnp.where(r16 == 0, part_a, 0.0)
        + jnp.where(r16 == 1, part_b, 0.0)
        + jnp.where(r16 == 2, part_c, 0.0)
    )

    def backward(n, _):
        at = pl.ds(pl.multiple_of(n * sub, sub), sub)
        d1 = jnp.zeros((TOP, sub), f32)
        d2 = jnp.zeros((96, sub), f32)
        for b in range(nblk):
            to = slice(b * BLOCK, (b + 1) * BLOCK)
            gp = (mm(qq[to, :], ww[:, at]) * der[to, at].astype(f32)).astype(bf16)
            d1 = d1 + mm(pt_refs[b][...], gp)
            d2 = d2 + mm(qqt[b], hid[to, at])
        d2 = d2[0:48] + d2[48:96]
        extra = jnp.where(n == 0, scal, 0.0)
        upper = d1[0:HALF]
        lower = jnp.concatenate([d1[HALF:96], d1[96:TOP] + extra, d2], axis=0)
        keep_ref[:, at] = jnp.where(first, upper, lower)
        send_ref[:, at] = jnp.where(first, lower, upper)
        return 0

    lax.fori_loop(0, hidden // sub, backward, 0)


def add_core_kernel(keep_ref, got_ref, g0_ref, s1_ref, s2_ref, s3_ref):
    n = g0_ref.shape[1]
    g0_ref[...] = keep_ref[:, 0:n] + got_ref[:, 0:n]
    for k, out in enumerate((s1_ref, s2_ref, s3_ref)):
        at = slice((k + 1) * n, (k + 2) * n)
        out[...] = (keep_ref[:, at] + got_ref[:, at]).astype(bf16)


def add_plane_kernel(g0_ref, r1_ref, r2_ref, r3_ref, out_ref):
    out_ref[...] = (
        g0_ref[...] + r1_ref[...].astype(f32) + r2_ref[...].astype(f32) + r3_ref[...].astype(f32)
    ).astype(bf16)


def add_line_kernel(h_ref, z1_ref, z2_ref, z3_ref, out_ref):
    for s in range(4):
        here, one, two, three = (
            ref[:, (s ^ k) * LANES : ((s ^ k) + 1) * LANES].astype(f32)
            for k, ref in enumerate((h_ref, z1_ref, z2_ref, z3_ref))
        )
        out_ref[:, s * LANES : (s + 1) * LANES] = ((here + one) + (two + three)).astype(bf16)


def step_kernel(fan_in, classes, *refs):
    own = refs[0:4]
    other = refs[4:8]
    (
        w1t, w2t, b1, b2, l1, r1t, l2, r2, l1_root, r1t_root, l2_root, r2_root, m1, v1, m2, v2,
    ) = refs[8:24]
    (
        loss_o, count_o, norm_o, grad1_o, grad2_o, w1_o, w2_o, l1_o, r1_o, l2_o, r2_o,
        m1_o, v1_o, b1_o, m2_o, v2_o, b2_o,
    ) = refs[24:41]
    g = refs[41]
    chip = lax.axis_index("dp")
    core = lax.axis_index("shard")
    first = core == 0
    half = LANES // 2
    scal = jnp.zeros((16, LANES), f32)
    for k in range(4):
        for s in range(4):
            at = slice(s * LANES, (s + 1) * LANES)
            mine = own[k][:, at].astype(f32)
            theirs = other[k][:, at].astype(f32)
            upper = jnp.where(first, mine, theirs)
            lower = jnp.where(first, theirs, mine)
            scal += lower[16:32]
            to = pl.ds(pl.multiple_of((chip ^ (s * 4 + k)) * LANES, LANES), LANES)
            g[0:HALF, to] = upper.astype(bf16)
            g[HALF:96, to] = lower[0:16].astype(bf16)
            keep = lax.broadcasted_iota(jnp.int32, (16, LANES), 0) <= fan_in - 96
            g[96:TOP, to] = jnp.where(keep, lower[16:32], 0.0).astype(bf16)
            g[TOP:ROWS, to] = lower[32:80].astype(bf16)
    row16 = lax.broadcasted_iota(jnp.int32, (16, LANES), 0)
    scal = jnp.where((row16 >= 5) & (row16 <= 10), scal, 0.0)
    vec = jnp.sum(scal, axis=0, keepdims=True)
    pos = lax.broadcasted_iota(jnp.int32, (1, LANES), 1)
    loss = jnp.sum(jnp.where(pos == 48, vec, 0.0), axis=1, keepdims=True)
    count = jnp.sum(jnp.where(pos == 49, vec, 0.0), axis=1, keepdims=True)
    inv = 1.0 / jnp.maximum(count, 1.0)
    gb2 = jnp.where(pos < classes, vec, 0.0) * inv
    whole = g[...]
    gram = mm(whole, whole, NT)
    gi = lax.broadcasted_iota(jnp.int32, gram.shape, 0)
    gj = lax.broadcasted_iota(jnp.int32, gram.shape, 1)
    squares = jnp.sum(jnp.where(gi == gj, gram, 0.0), axis=0, keepdims=True)
    squares = jnp.sum(squares, axis=1, keepdims=True) * inv * inv
    squares = squares + jnp.sum(gb2 * gb2, axis=1, keepdims=True)
    norm = jnp.sqrt(squares)
    factor = jnp.minimum(1.0, clip_limit / (norm + 1e-06))
    s = factor * inv
    ss = (1.0 - beta_stat) * s * s
    loss_o[...] = loss
    count_o[...] = count
    norm_o[...] = norm
    l1_o[...] = beta_stat * l1[...] + ss * gram[0:fan_in, 0:fan_in]
    g2t = g[TOP:ROWS, :]
    r2_o[...] = beta_stat * r2[...] + ss * mm(g2t, g2t, NT)[0:classes, 0:classes]

    mine = g[:, pl.ds(pl.multiple_of(chip * LANES, LANES), LANES)].astype(f32)
    mine = jnp.where(first, mine, pltpu.roll(mine, half, 1))[:, 0:half]
    mine_b = mine.astype(bf16)
    eye = (
        lax.broadcasted_iota(jnp.int32, (half, half), 0)
        == lax.broadcasted_iota(jnp.int32, (half, half), 1)
    ).astype(bf16)
    mine_t = mm(eye, mine_b, NT)
    own1_t = mine_t[:, 0:TOP].astype(bf16)
    grad1_o[...] = s * mine_t[:, 0:fan_in]
    grad2_o[...] = s * mine[TOP : TOP + classes, :]
    own2 = mm(eye, mine_b[TOP:ROWS], NT).astype(bf16)
    g1 = g[0:TOP, :]
    zero_bias = lax.broadcasted_iota(jnp.int32, own1_t.shape, 1) < fan_in
    own1_t = jnp.where(zero_bias, own1_t.astype(f32), 0.0).astype(bf16)
    r1_o[...] = beta_stat * r1t[...] + ss * mm(own1_t, g1)
    l2_o[...] = beta_stat * l2[...] + ss * mm(own2, g2t)
    t1 = mm(r1t_root[...].astype(bf16), g1, NT)[:, 0:fan_in]
    t1 = lax.dot_general(t1, l1_root[...], NT, precision=highest, preferred_element_type=f32)
    w1_o[...] = w1t[...] - (rate_first * s) * t1
    t2 = mm(l2_root[...].astype(bf16), g2t, NT)[:, 0:classes]
    t2 = lax.dot_general(
        r2_root[...], t2, (((0,), (1,)), ((), ())), precision=highest, preferred_element_type=f32
    )
    w2_o[...] = w2t[...] - (rate_second * s) * t2
    m1_o[...], v1_o[...], b1_o[...] = adam_step(
        b1[...], s * mine[fan_in : fan_in + 1, :], m1[...], v1[...]
    )
    m2_o[...], v2_o[...], b2_o[...] = adam_step(
        b2[...], factor * gb2[:, 0:classes], m2[...], v2[...]
    )


def swap(array, bits):
    count = lax.axis_size(AXES)
    return lax.ppermute(array, AXES, [(i, i ^ bits) for i in range(count)])


def fast_device(
    features, neighbors, label_mask, labels, w_first, w_second, b_first, b_second, l_first, r_first,
    l_second, r_second, l_first_root, r_first_root, l_second_root, r_second_root, m_first, v_first,
    m_second, v_second,
):
    fan_in, width = w_first.shape
    classes = w_second.shape[1]
    degree = neighbors.shape[1]
    nblk = features.shape[0] // BLOCK
    hidden = width * lax.axis_size(AXES)
    group = hidden // 4
    shape = jax.ShapeDtypeStruct
    w1t, w2t, b1 = w_first.T, w_second.T, b_first.reshape(1, width)

    piece = pl.pallas_call(
        pack_kernel,
        out_shape=shape((HALF, LANES), bf16),
        scratch_shapes=[pltpu.VMEM((HALF, width), f32)],
        compiler_params=params(8),
        cost_estimate=cost(1),
        name="pack",
    )(w1t, w2t, b1)
    line = jnp.concatenate([piece] + [swap(piece, 8 * k) for k in (1, 2, 3)], axis=1)
    plane = [line] + [swap(line, 2 * k) for k in (1, 2, 3)]
    partner = [swap(part, 1) for part in plane]

    graphs = []
    nbr_t, feat_t = neighbors.T, features.T
    for b in range(nblk):
        graphs.append(
            pl.pallas_call(
                functools.partial(graph_kernel, fan_in),
                grid=(1,),
                in_specs=[
                    pl.BlockSpec((degree, BLOCK), lambda i, b=b: (0, b)),
                    pl.BlockSpec((fan_in, BLOCK), lambda i, b=b: (0, b)),
                ],
                out_specs=[
                    pl.BlockSpec((BLOCK, BLOCK), lambda i: (0, 0)),
                    pl.BlockSpec((BLOCK, LANES), lambda i: (0, 0)),
                    pl.BlockSpec((TOP, BLOCK), lambda i: (0, 0)),
                ],
                out_shape=[
                    shape((BLOCK, BLOCK), bf16),
                    shape((BLOCK, LANES), bf16),
                    shape((TOP, BLOCK), bf16),
                ],
                compiler_params=params(24),
                cost_estimate=cost(3),
                name="graph",
            )(nbr_t, feat_t)
        )
    ms = [graph[0] for graph in graphs]
    ps = [graph[1] for graph in graphs]
    pts = [graph[2] for graph in graphs]

    vmem = pl.BlockSpec(memory_space=pltpu.VMEM)
    keep, send = pl.pallas_call(
        functools.partial(main_kernel, nblk, classes, degree),
        in_specs=[vmem] * 8 + [pl.BlockSpec(memory_space=pl.ANY)] * nblk + [vmem] * (2 * nblk + 3),
        out_specs=[vmem, vmem],
        out_shape=[shape((HALF, hidden), f32)] * 2,
        scratch_shapes=[
            pltpu.VMEM((ROWS, hidden), bf16),
            pltpu.VMEM((LANES, hidden), bf16),
            pltpu.VMEM((nblk * BLOCK, hidden), bf16),
            pltpu.VMEM((nblk * BLOCK, hidden), bf16),
            pltpu.VMEM((nblk, BLOCK, BLOCK), bf16),
            pltpu.VMEM((nblk * BLOCK, LANES), f32),
            pltpu.VMEM((nblk * BLOCK, LANES), bf16),
            pltpu.VMEM((nblk, 96, BLOCK), bf16),
            pltpu.VMEM((8, 256), f32),
            pltpu.SemaphoreType.DMA((nblk,)),
        ],
        compiler_params=params(),
        cost_estimate=cost(15),
        name="main",
    )(
        *plane,
        *partner,
        *ms,
        *ps,
        *pts,
        label_mask.reshape(nblk, BLOCK),
        labels.reshape(nblk, BLOCK),
        jnp.pad(b_second, (0, 48 - classes)).reshape(48, 1),
    )

    got = swap(send, 1)
    g0, s1, s2, s3 = pl.pallas_call(
        add_core_kernel,
        out_shape=[shape((HALF, group), f32)] + [shape((HALF, group), bf16)] * 3,
        compiler_params=params(16),
        cost_estimate=cost(1),
        name="add_core",
    )(keep, got)
    mine = pl.pallas_call(
        add_plane_kernel,
        out_shape=shape((HALF, group), bf16),
        compiler_params=params(8),
        cost_estimate=cost(1),
        name="add_plane",
    )(g0, swap(s1, 2), swap(s2, 4), swap(s3, 6))
    mine = pl.pallas_call(
        add_line_kernel,
        out_shape=shape((HALF, group), bf16),
        compiler_params=params(8),
        cost_estimate=cost(1),
        name="add_line",
    )(mine, swap(mine, 8), swap(mine, 16), swap(mine, 24))
    plane = [mine] + [swap(mine, 2 * k) for k in (1, 2, 3)]
    partner = [swap(part, 1) for part in plane]

    one = shape((1, 1), f32)
    row1, row2 = shape((1, width), f32), shape((1, classes), f32)
    outs = pl.pallas_call(
        functools.partial(step_kernel, fan_in, classes),
        out_shape=[
            one, one, one, shape(w1t.shape, f32), shape(w2t.shape, f32), shape(w1t.shape, f32),
            shape(w2t.shape, f32), shape(l_first.shape, f32), shape((width, hidden), f32),
            shape((width, hidden), f32), shape(r_second.shape, f32),
            row1, row1, row1, row2, row2, row2,
        ],
        scratch_shapes=[pltpu.VMEM((ROWS, hidden), bf16)],
        compiler_params=params(32),
        cost_estimate=cost(5),
        name="update",
    )(
        *plane,
        *partner,
        w1t, w2t, b1, b_second.reshape(1, classes), l_first, r_first.T, l_second, r_second,
        l_first_root, r_first_root.T, l_second_root, r_second_root,
        m_first.reshape(1, width), v_first.reshape(1, width),
        m_second.reshape(1, classes), v_second.reshape(1, classes),
    )
    loss, count, norm, grad1, grad2, w1, w2, l1, r1, l2, r2, m1, v1, nb1, m2, v2, nb2 = outs
    return (
        loss.reshape(()), count.reshape(()), norm.reshape(()), grad1.T, grad2.T, w1.T, w2.T,
        l1, r1.T, l2, r2, m1.reshape(width), v1.reshape(width), nb1.reshape(width),
        m2.reshape(classes), v2.reshape(classes), nb2.reshape(classes),
    )


def general_device(
    features, neighbors, label_mask, labels, w_first, w_second, b_first, b_second, l_first, r_first,
    l_second, r_second, l_first_root, r_first_root, l_second_root, r_second_root, m_first, v_first,
    m_second, v_second,
):
    fan_in, width = w_first.shape
    classes = w_second.shape[1]
    scale_in = 1.0 / (neighbors.shape[1] + 1)
    packed = jnp.concatenate([w_first, b_first[None, :], w_second.T], axis=0).astype(bf16)
    packed = lax.all_gather(packed, AXES, axis=1, tiled=True)
    first_full, bias_full, second_full = packed[:fan_in], packed[fan_in], packed[fan_in + 1 :]
    loss = jnp.zeros((), f32)
    grads = jnp.zeros(packed.shape, f32)
    gb2 = jnp.zeros_like(b_second)
    for b in range(features.shape[0] // BLOCK):
        at = slice(b * BLOCK, (b + 1) * BLOCK)
        columns = jnp.arange(BLOCK, dtype=jnp.int32)
        counts = jnp.sum(
            (neighbors[at][:, :, None] == columns[None, None, :]).astype(f32), axis=1
        )
        eye = jnp.eye(BLOCK, dtype=f32)
        matrix = (counts + eye * (2.0 + jnp.sum(counts * eye, axis=1))[:, None]).astype(bf16)
        pooled = (mm(matrix, features[at]) * scale_in).astype(bf16)
        pre = mm(pooled, first_full) + bias_full.astype(f32)
        hidden = jax.nn.gelu(pre).astype(bf16)
        logits = (
            jnp.dot(matrix.astype(f32), mm(hidden, second_full, NT), precision=highest) * scale_in
            + b_second
        )
        log_prob = jax.nn.log_softmax(logits, axis=-1)
        onehot = (labels[at][:, None] == jnp.arange(classes, dtype=jnp.int32)[None, :]).astype(f32)
        weight = label_mask[at].astype(f32)
        loss = loss - jnp.sum(jnp.sum(log_prob * onehot, axis=-1) * weight)
        grad = ((jnp.exp(log_prob) - onehot) * weight[:, None]).astype(bf16)
        gb2 = gb2 + jnp.sum(grad.astype(f32), axis=0)
        back = (mm(matrix, grad, TN) * scale_in).astype(bf16)
        grad_pre = jax.vjp(jax.nn.gelu, pre)[1](mm(back, second_full))[0].astype(bf16)
        grads = grads + jnp.concatenate(
            [
                mm(pooled, grad_pre, TN),
                jnp.sum(grad_pre.astype(f32), axis=0, keepdims=True),
                mm(back, hidden, TN),
            ],
            axis=0,
        )
    count = jnp.sum(label_mask).astype(f32)
    grads, gb2, loss, count = lax.psum((grads, gb2, loss, count), AXES)
    inv = 1.0 / jnp.maximum(count, 1.0)
    grads, gb2 = grads * inv, gb2 * inv
    norm = jnp.sqrt(jnp.sum(grads * grads) + jnp.sum(gb2 * gb2))
    factor = jnp.minimum(1.0, clip_limit / (norm + 1e-06))
    grads, gb2 = grads * factor, gb2 * factor
    at = lax.axis_index(AXES) * width
    own = lax.dynamic_slice_in_dim(grads, at, width, axis=1)
    full_one, full_two = grads[:fan_in], grads[fan_in + 1 :].T
    own_one, own_bias, own_two = own[:fan_in], own[fan_in], own[fan_in + 1 :].T
    dot = functools.partial(jnp.dot, precision=highest)
    keep, add = beta_stat, 1.0 - beta_stat
    m1, v1, b1 = adam_step(b_first, own_bias, m_first, v_first)
    m2, v2, b2 = adam_step(b_second, gb2, m_second, v_second)
    return (
        loss, count, norm, own_one, own_two,
        w_first - rate_first * dot(l_first_root, dot(full_one, r_first_root)),
        w_second - rate_second * dot(dot(l_second_root, full_two), r_second_root),
        keep * l_first + add * dot(full_one, full_one.T),
        keep * r_first + add * dot(full_one.T, own_one),
        keep * l_second + add * dot(own_two, full_two.T),
        keep * r_second + add * dot(full_two.T, full_two),
        m1, v1, b1, m2, v2, b2,
    )


def solution(mesh):
    split0 = P(AXES)
    rows = P(AXES, None)
    columns = P(None, AXES)
    whole = P()
    fast = mesh.shape["dp"] == 16 and mesh.shape["shard"] == 2

    def per_device(*args):
        width = args[4].shape[1]
        return (fast_device if fast and 2 * width == LANES else general_device)(*args)

    return jax.shard_map(
        per_device,
        mesh=mesh,
        in_specs=(
            rows, rows, split0, split0, columns, rows, split0, whole, whole, columns, rows, whole,
            whole, columns, rows, whole, split0, split0, whole, whole,
        ),
        out_specs=(
            whole, whole, whole, columns, rows, columns, rows, whole, columns, rows, whole,
            split0, split0, split0, whole, whole, whole,
        ),
        check_vma=False,
    )
```

```python
import functools

import jax
import jax.numpy as jnp
from jax import lax
from jax.experimental import pallas as pl
from jax.experimental.pallas import tpu as pltpu
from jax.sharding import PartitionSpec as P

STEP = 10
BLOCK = 1024
AXES = ("dp", "shard")

clip_limit = 0.05
beta_stat = 0.95
beta_one = 0.9
beta_two = 0.999
adam_eps = 1e-08
decay_rate = 0.01
rate_bias = 0.2
rate_first = 1000.0
rate_second = 300.0
highest = lax.Precision.HIGHEST

f32 = jnp.float32
bf16 = jnp.bfloat16
NN = (((1,), (0,)), ((), ()))
NT = (((1,), (1,)), ((), ()))
TN = (((0,), (0,)), ((), ()))

ROWS = 160
HALF = 80
TOP = 112
LANES = 128


def mm(a, b, dims=NN):
    return lax.dot_general(a, b, dims, preferred_element_type=f32)


def call(kernel, name, us, limit, out_shape, *args, after=(), scratch=(), **kw):
    n = len(args)

    def body(*refs):
        kernel(*refs[:n], *refs[n + len(after) :])

    kw.setdefault("in_specs", [pl.BlockSpec(memory_space=pltpu.VMEM)] * n)
    kw["in_specs"] = list(kw["in_specs"]) + [pl.BlockSpec(memory_space=pl.ANY)] * len(after)
    return pl.pallas_call(
        body,
        out_shape=out_shape,
        scratch_shapes=scratch,
        compiler_params=pltpu.CompilerParams(vmem_limit_bytes=limit * 2**20),
        cost_estimate=pl.CostEstimate(
            flops=int(us * 1e9), bytes_accessed=int(us * 2e6), transcendentals=0
        ),
        name=name,
        **kw,
    )(*args, *after)


def adam_step(param, grad, first, second):
    first_new = beta_one * first + (1.0 - beta_one) * grad
    second_new = beta_two * second + (1.0 - beta_two) * grad * grad
    corr_one = 1.0 - beta_one**STEP
    corr_two = 1.0 - beta_two**STEP
    update = (
        first_new / corr_one / (jnp.sqrt(second_new / corr_two) + adam_eps) + decay_rate * param
    )
    return (first_new, second_new, param - rate_bias * update)


def pack_kernel(w1t_hbm, w2t_hbm, b_hbm, out_ref, w1t_ref, w2t_ref, b_ref, bottom, sem):
    copies = [
        pltpu.make_async_copy(source, target, sem.at[k])
        for k, (source, target) in enumerate(
            ((w1t_hbm, w1t_ref), (w2t_hbm, w2t_ref), (b_hbm, b_ref))
        )
    ]
    for copy in copies:
        copy.start()
    for copy in copies:
        copy.wait()
    fan_in = w1t_ref.shape[1]
    width = w1t_ref.shape[0]
    classes = w2t_ref.shape[0]
    rows = lax.broadcasted_iota(jnp.int32, (TOP, fan_in), 0)
    cols = lax.broadcasted_iota(jnp.int32, (TOP, fan_in), 1)
    eye = (rows == cols).astype(bf16)
    w1 = mm(eye, w1t_ref[...].astype(bf16), NT)
    rows = lax.broadcasted_iota(jnp.int32, (TOP, width), 0)
    w1 = jnp.where(rows == fan_in, b_ref[...], w1)
    out_ref[:, 0:width] = w1[0:HALF].astype(bf16)
    bottom[...] = jnp.zeros_like(bottom)
    bottom[0 : TOP - HALF, :] = w1[HALF:TOP]
    bottom[TOP - HALF : TOP - HALF + classes, :] = w2t_ref[...]
    out_ref[:, width : 2 * width] = bottom[...].astype(bf16)


def graph_kernel(fan_in, block, nbr_ref, feat_ref, m_ref, p_ref, pt_ref):
    classes = nbr_ref.shape[0]
    scale_in = 1.0 / (classes + 1)
    base = lax.broadcasted_iota(jnp.int32, (16, LANES), 0).astype(jnp.int16)
    one = jnp.ones((16, LANES), bf16)
    zero = jnp.zeros((16, LANES), bf16)
    row = lax.broadcasted_iota(jnp.int32, (LANES, LANES), 0)
    col = lax.broadcasted_iota(jnp.int32, (LANES, LANES), 1)
    base_at = block * BLOCK
    for t in range(BLOCK // LANES):
        at = slice(t * LANES, (t + 1) * LANES)
        slots = [
            jnp.broadcast_to(nbr_ref[k : k + 1, base_at + t * LANES : base_at + (t + 1) * LANES], (16, LANES)).astype(jnp.int16)
            for k in range(classes)
        ]
        for u in range(BLOCK // 16):
            here = base + jnp.int16(u * 16)
            terms = [jnp.where(s == here, one, zero) for s in slots]
            while len(terms) > 1:
                terms = [sum(terms[a : a + 2][1:], terms[a]) for a in range(0, len(terms), 2)]
            m_ref[u * 16 : (u + 1) * 16, at] = terms[0]
        square = m_ref[at, at].astype(f32)
        m_ref[at, at] = jnp.where(row == col, 2.0 * square + 2.0, square).astype(bf16)
    pooled = mm(feat_ref[:, base_at : base_at + BLOCK], m_ref[...]) * scale_in
    rest = LANES - fan_in - 1
    pooled = jnp.concatenate(
        [pooled, jnp.ones((1, BLOCK), f32), jnp.zeros((rest, BLOCK), f32)], axis=0
    )
    pt_ref[...] = pooled[0:TOP].astype(bf16)
    p_ref[...] = pooled.T.astype(bf16)


def forward_kernel(nblk, *refs):
    own_ref, other_ref = refs[0:2]
    p_refs = refs[2 : 2 + nblk]
    ww, hid, der, zt, w = refs[2 + nblk :]
    group = w.shape[1]
    first = lax.axis_index("shard") == 0

    left = lax.broadcasted_iota(jnp.int32, (HALF, LANES), 1) < LANES // 2
    row = lax.broadcasted_iota(jnp.int32, (HALF, LANES), 0)
    for s in range(group // LANES):
        at = slice(s * LANES, (s + 1) * LANES)
        mine = own_ref[:, at].astype(f32)
        theirs = other_ref[:, at].astype(f32)
        lo = jnp.where(first, mine, theirs)
        hi = jnp.where(first, theirs, mine)
        upper = jnp.where(left, lo, pltpu.roll(hi, LANES // 2, 1))
        lower = jnp.where(left, pltpu.roll(lo, LANES // 2, 1), hi)
        w[0:HALF, at] = (0.5 * upper).astype(bf16)
        w[HALF:ROWS, at] = jnp.where(row < TOP - HALF, 0.5 * lower, lower).astype(bf16)
    ww[0:48, :] = w[TOP:ROWS, :]
    ww[48:96, :] = w[TOP:ROWS, :]
    ww[96:128, :] = jnp.zeros((32, group), bf16)

    c0 = 0.7978845608028654
    c1 = c0 * 0.044715
    narrow = 256
    for n in range(group // narrow):
        at = slice(n * narrow, (n + 1) * narrow)
        for b in range(nblk):
            to = slice(b * BLOCK, (b + 1) * BLOCK)
            x = mm(p_refs[b][...], w[0:LANES, at])
            xb = x.astype(bf16)
            k = bf16(8.0 * c1) * (xb * xb)
            s = bf16(1.0) + jnp.tanh(xb * (k + bf16(2.0 * c0)))
            hb = xb * s
            d = s + ((bf16(2.0) - s) * hb) * (bf16(3.0) * k + bf16(2.0 * c0))
            hid[to, at] = hb
            der[to, at] = d.astype(bf16)
            part = mm(w[TOP:ROWS, at], hb, NT)
            zt[b] = part if n == 0 else zt[b] + part


def middle_kernel(nblk, classes, degree, *refs):
    z_refs = refs[0:4]
    m_refs = refs[4 : 4 + nblk]
    mask_ref, label_ref, b2_ref = refs[4 + nblk : 7 + nblk]
    qq, qqt, scal_ref, row_scr = refs[7 + nblk :]
    first = lax.axis_index("shard") == 0
    scale_in = 1.0 / (degree + 1)
    pick = lax.broadcasted_iota(jnp.int32, (48, classes), 0) == lax.broadcasted_iota(
        jnp.int32, (48, classes), 1
    )
    bias = jnp.sum(jnp.where(pick, b2_ref[...], 0.0), axis=1, keepdims=True)
    row_scr[...] = jnp.zeros_like(row_scr)
    loss = jnp.zeros((1, 1), f32)
    count = jnp.zeros((1, 1), f32)
    for b in range(nblk):
        zb = (z_refs[0][b] + z_refs[1][b]) + (z_refs[2][b] + z_refs[3][b])
        z_hi = zb.astype(bf16)
        z_lo = (zb - z_hi.astype(f32)).astype(bf16)
        both = mm(jnp.concatenate([z_hi, z_lo], axis=0), m_refs[b][...])
        logits = (both[0:48] + both[48:96]) * scale_in + bias
        cls = lax.broadcasted_iota(jnp.int32, (48, BLOCK), 0)
        logits = jnp.where(cls < classes, logits, -1e30)
        top = jnp.max(logits, axis=0, keepdims=True)
        e = jnp.exp(logits - top)
        total = jnp.sum(e, axis=0, keepdims=True)
        mine = slice(b * BLOCK, (b + 1) * BLOCK)
        hit = cls == label_ref[mine].reshape(1, BLOCK)
        weight = mask_ref[mine].reshape(1, BLOCK).astype(f32)
        picked = jnp.sum(jnp.where(hit, logits, 0.0), axis=0, keepdims=True)
        loss += jnp.sum((jnp.log(total) + top - picked) * weight, axis=1, keepdims=True)
        count += jnp.sum(weight, axis=1, keepdims=True)
        grad = ((e / total - hit.astype(f32)) * weight).astype(bf16)
        row_scr[:, 0:48] += mm(jnp.ones((8, BLOCK), bf16), grad, NT)
        q = mm(grad, m_refs[b][...], NT) * scale_in
        q_hi = q.astype(bf16)
        q_lo = q - q_hi.astype(f32)
        q2 = jnp.concatenate([q_hi.astype(f32), q_lo, jnp.zeros((32, BLOCK), f32)], axis=0)
        qqt[b] = q2[0:96].astype(bf16)
        qq[b * BLOCK : (b + 1) * BLOCK, :] = (0.5 * q2).T.astype(bf16)

    vec = row_scr[0:1, :]
    pos = lax.broadcasted_iota(jnp.int32, vec.shape, 1)
    vec = jnp.where(pos == 48, loss, jnp.where(pos == 49, count, vec))
    part_a = vec.astype(bf16).astype(f32)
    part_b = (vec - part_a).astype(bf16).astype(f32)
    part_c = (vec - part_a - part_b).astype(bf16).astype(f32)
    r16 = lax.broadcasted_iota(jnp.int32, (16, LANES), 0) - jnp.where(first, 5, 8)
    scal_ref[...] = (
        jnp.where(r16 == 0, part_a, 0.0)
        + jnp.where(r16 == 1, part_b, 0.0)
        + jnp.where(r16 == 2, part_c, 0.0)
    )


def backward_kernel(nblk, has_scalars, *refs):
    qq, qqt = refs[0:2]
    pt_refs = refs[2 : 2 + nblk]
    ww, hid, der, scal_ref = refs[2 + nblk : 6 + nblk]
    keep_ref, send_ref = refs[6 + nblk :]
    first = lax.axis_index("shard") == 0
    group = ww.shape[1]
    d1 = jnp.zeros((TOP, group), f32)
    d2 = jnp.zeros((96, group), f32)
    for b in range(nblk):
        to = slice(b * BLOCK, (b + 1) * BLOCK)
        gp = (mm(qq[to, :], ww[...]) * der[to, :].astype(f32)).astype(bf16)
        d1 = d1 + mm(pt_refs[b][...], gp)
        d2 = d2 + mm(qqt[b], hid[to, :])
    d2 = d2[0:48] + d2[48:96]
    upper = d1[0:HALF]
    middle = d1[96:TOP]
    if has_scalars:
        middle += jnp.concatenate([scal_ref[...], jnp.zeros((16, group - LANES), f32)], axis=1)
    lower = jnp.concatenate([d1[HALF:96], middle, d2], axis=0)
    keep_ref[...] = jnp.where(first, upper, lower)
    send_ref[...] = jnp.where(first, lower, upper)


def add_core_kernel(*refs):
    keeps, gots, outs = refs[0:4], refs[4:8], refs[8:12]
    first = lax.axis_index("shard") == 0
    total = [
        [
            keep[:, u * LANES : (u + 1) * LANES] + got[:, u * LANES : (u + 1) * LANES]
            for u in range(4)
        ]
        for keep, got in zip(keeps, gots, strict=True)
    ]
    for k, out in enumerate(outs):
        for u in range(4):
            picked = jnp.where(first, total[k][u], total[u][k])
            out[:, u * LANES : (u + 1) * LANES] = picked.astype(out.dtype)


def add_piece_kernel(own_ref, r1_ref, r2_ref, r3_ref, out_ref):
    out_ref[...] = (
        own_ref[...] + r1_ref[...].astype(f32) + r2_ref[...].astype(f32) + r3_ref[...].astype(f32)
    ).astype(bf16)


def add_line_kernel(h_ref, z1_ref, z2_ref, z3_ref, out_ref):
    for s in range(4):
        here, one, two, three = (
            ref[:, (s ^ k) * LANES : ((s ^ k) + 1) * LANES].astype(f32)
            for k, ref in enumerate((h_ref, z1_ref, z2_ref, z3_ref))
        )
        out_ref[:, s * LANES : (s + 1) * LANES] = ((here + one) + (two + three)).astype(bf16)


def step_kernel(fan_in, classes, *refs):
    own = refs[0:4]
    other = refs[4:8]
    (
        w1t, w2t, b1, b2, l1, r1t, l2, r2, l1_root, r1t_root, l2_root, r2_root, m1, v1, m2, v2,
    ) = refs[8:24]
    (
        loss_o, count_o, norm_o, grad1_o, grad2_o, w1_o, w2_o, l1_o, r1_o, l2_o, r2_o,
        m1_o, v1_o, b1_o, m2_o, v2_o, b2_o,
    ) = refs[24:41]
    g = refs[41]
    chip = lax.axis_index("dp")
    core = lax.axis_index("shard")
    first = core == 0
    half = LANES // 2
    for refs_of, owner in ((own, core), (other, 1 - core)):
        rows = pl.ds(pl.multiple_of(owner * HALF, 16), HALF)
        for k in range(4):
            for u in range(4):
                slot = jnp.where(owner == 0, u * 4 + k, k * 4 + u)
                to = pl.ds(pl.multiple_of((chip ^ slot) * LANES, LANES), LANES)
                g[rows, to] = refs_of[k][:, u * LANES : (u + 1) * LANES]
    mixed = g[96:TOP, :].astype(f32)
    scal = sum(mixed[:, u * LANES : (u + 1) * LANES] for u in range(mixed.shape[1] // LANES))
    keep = lax.broadcasted_iota(jnp.int32, mixed.shape, 0) <= fan_in - 96
    g[96:TOP, :] = jnp.where(keep, mixed, 0.0).astype(bf16)
    row16 = lax.broadcasted_iota(jnp.int32, (16, LANES), 0)
    scal = jnp.where((row16 >= 5) & (row16 <= 10), scal, 0.0)
    vec = jnp.sum(scal, axis=0, keepdims=True)
    pos = lax.broadcasted_iota(jnp.int32, (1, LANES), 1)
    loss = jnp.sum(jnp.where(pos == 48, vec, 0.0), axis=1, keepdims=True)
    count = jnp.sum(jnp.where(pos == 49, vec, 0.0), axis=1, keepdims=True)
    inv = 1.0 / jnp.maximum(count, 1.0)
    gb2 = jnp.where(pos < classes, vec, 0.0) * inv
    whole = g[...]
    gram = mm(whole, whole, NT)
    gi = lax.broadcasted_iota(jnp.int32, gram.shape, 0)
    gj = lax.broadcasted_iota(jnp.int32, gram.shape, 1)
    squares = jnp.sum(jnp.where(gi == gj, gram, 0.0), axis=0, keepdims=True)
    squares = jnp.sum(squares, axis=1, keepdims=True) * inv * inv
    squares = squares + jnp.sum(gb2 * gb2, axis=1, keepdims=True)
    norm = jnp.sqrt(squares)
    factor = jnp.minimum(1.0, clip_limit / (norm + 1e-06))
    s = factor * inv
    ss = (1.0 - beta_stat) * s * s
    loss_o[...] = loss
    count_o[...] = count
    norm_o[...] = norm
    l1_o[...] = beta_stat * l1[...] + ss * gram[0:fan_in, 0:fan_in]
    g2t = g[TOP:ROWS, :]
    r2_o[...] = beta_stat * r2[...] + ss * mm(g2t, g2t, NT)[0:classes, 0:classes]

    mine = g[:, pl.ds(pl.multiple_of(chip * LANES, LANES), LANES)].astype(f32)
    mine = jnp.where(first, mine, pltpu.roll(mine, half, 1))[:, 0:half]
    mine_b = mine.astype(bf16)
    eye = (
        lax.broadcasted_iota(jnp.int32, (half, half), 0)
        == lax.broadcasted_iota(jnp.int32, (half, half), 1)
    ).astype(bf16)
    mine_t = mm(eye, mine_b, NT)
    own1_t = mine_t[:, 0:TOP].astype(bf16)
    grad1_o[...] = s * mine_t[:, 0:fan_in]
    grad2_o[...] = s * mine[TOP : TOP + classes, :]
    own2 = mm(eye, mine_b[TOP:ROWS], NT).astype(bf16)
    g1 = g[0:TOP, :]
    zero_bias = lax.broadcasted_iota(jnp.int32, own1_t.shape, 1) < fan_in
    own1_t = jnp.where(zero_bias, own1_t.astype(f32), 0.0).astype(bf16)
    r1_o[...] = beta_stat * r1t[...] + ss * mm(own1_t, g1)
    l2_o[...] = beta_stat * l2[...] + ss * mm(own2, g2t)
    t1 = mm(r1t_root[...].astype(bf16), g1, NT)[:, 0:fan_in]
    t1 = lax.dot_general(t1, l1_root[...], NT, precision=highest, preferred_element_type=f32)
    w1_o[...] = w1t[...] - (rate_first * s) * t1
    t2 = mm(l2_root[...].astype(bf16), g2t, NT)[:, 0:classes]
    t2 = lax.dot_general(
        r2_root[...], t2, (((0,), (1,)), ((), ())), precision=highest, preferred_element_type=f32
    )
    w2_o[...] = w2t[...] - (rate_second * s) * t2
    m1_o[...], v1_o[...], b1_o[...] = adam_step(
        b1[...], s * mine[fan_in : fan_in + 1, :], m1[...], v1[...]
    )
    m2_o[...], v2_o[...], b2_o[...] = adam_step(
        b2[...], factor * gb2[:, 0:classes], m2[...], v2[...]
    )


def swap(array, bits, bits_one=None):
    count = lax.axis_size(AXES)
    both = (bits, bits if bits_one is None else bits_one)
    return lax.ppermute(array, AXES, [(i, i ^ both[i % 2]) for i in range(count)])


def fast_device(
    features, neighbors, label_mask, labels, w_first, w_second, b_first, b_second, l_first, r_first,
    l_second, r_second, l_first_root, r_first_root, l_second_root, r_second_root, m_first, v_first,
    m_second, v_second,
):
    fan_in, width = w_first.shape
    classes = w_second.shape[1]
    degree = neighbors.shape[1]
    nblk = features.shape[0] // BLOCK
    hidden = width * lax.axis_size(AXES)
    group = hidden // 4
    shape = jax.ShapeDtypeStruct
    w1t, w2t, b1 = w_first.T, w_second.T, b_first.reshape(1, width)

    piece = call(
        pack_kernel, "pack", 1, 60, shape((HALF, LANES), bf16), w1t, w2t, b1,
        in_specs=[pl.BlockSpec(memory_space=pl.ANY)] * 3,
        scratch=[
            pltpu.VMEM(w1t.shape, f32),
            pltpu.VMEM(w2t.shape, f32),
            pltpu.VMEM(b1.shape, f32),
            pltpu.VMEM((HALF, width), f32),
            pltpu.SemaphoreType.DMA((3,)),
        ],
    )
    line = jnp.concatenate([piece] + [swap(piece, 8 * k) for k in (1, 2, 3)], axis=1)
    plane = [line] + [swap(line, 2 * k) for k in (1, 2, 3)]
    partner = [swap(line, 1)]

    nbr_t, feat_t = neighbors.T, features.T
    graphs = [
        call(
            functools.partial(graph_kernel, fan_in, b), "graph", 2.6, 4,
            [shape((BLOCK, BLOCK), bf16), shape((BLOCK, LANES), bf16), shape((TOP, BLOCK), bf16)],
            nbr_t, feat_t, after=[line] * (b > 0),
        )
        for b in range(nblk)
    ]
    ms, ps, pts = ([graph[k] for graph in graphs] for k in range(3))

    nodes = nblk * BLOCK
    fwd = []
    for g in range(4):
        if g:
            plane[g], _ = lax.optimization_barrier((plane[g], fwd[0][3]))
            partner.append(swap(plane[g], 1))
        fwd.append(
            call(
                functools.partial(forward_kernel, nblk), "forward", 2, 4,
                [
                    shape((LANES, group), bf16), shape((nodes, group), bf16),
                    shape((nodes, group), bf16), shape((nblk, 48, BLOCK), f32),
                ],
                plane[g], partner[g], *ps,
                scratch=[pltpu.VMEM((ROWS, group), bf16)],
            )
        )
    qq, qqt, scal = call(
        functools.partial(middle_kernel, nblk, classes, degree), "middle", 2.6, 4,
        [shape((nodes, LANES), bf16), shape((nblk, 96, BLOCK), bf16), shape((16, LANES), f32)],
        *[f[3] for f in fwd], *ms, label_mask, labels, b_second.reshape(1, classes),
        scratch=[pltpu.VMEM((8, LANES), f32)],
    )
    keeps, gots = [], []
    for g in range(4):
        keep, send = call(
            functools.partial(backward_kernel, nblk, g == 0), "backward", 1.4, 4,
            [shape((HALF, group), f32)] * 2,
            qq, qqt, *pts, *fwd[g][0:3], scal,
        )
        keeps.append(keep)
        gots.append(swap(send, 1))
    mine, *rest = call(
        add_core_kernel, "add_core", 0.3, 4,
        [shape((HALF, group), f32)] + [shape((HALF, group), bf16)] * 3, *keeps, *gots,
    )
    mine = call(
        add_piece_kernel, "add_piece", 0.3, 2, shape((HALF, group), bf16),
        mine, *[swap(rest[k - 1], 2 * k, 8 * k) for k in (1, 2, 3)],
    )
    mine = call(
        add_line_kernel, "add_line", 0.3, 2, shape((HALF, group), bf16),
        mine, *[swap(mine, 8 * k, 2 * k) for k in (1, 2, 3)],
    )
    plane = [mine] + [swap(mine, 2 * k, 8 * k) for k in (1, 2, 3)]
    partner = [swap(part, 1) for part in plane]

    one = shape((1, 1), f32)
    row1, row2 = shape((1, width), f32), shape((1, classes), f32)
    outs = call(
        functools.partial(step_kernel, fan_in, classes), "update", 2.5, 8,
        [
            one, one, one, shape(w1t.shape, f32), shape(w2t.shape, f32), shape(w1t.shape, f32),
            shape(w2t.shape, f32), shape(l_first.shape, f32), shape((width, hidden), f32),
            shape((width, hidden), f32), shape(r_second.shape, f32),
            row1, row1, row1, row2, row2, row2,
        ],
        *plane, *partner,
        w1t, w2t, b1, b_second.reshape(1, classes), l_first, r_first.T, l_second, r_second,
        l_first_root, r_first_root.T, l_second_root, r_second_root,
        m_first.reshape(1, width), v_first.reshape(1, width),
        m_second.reshape(1, classes), v_second.reshape(1, classes),
        scratch=[pltpu.VMEM((ROWS, hidden), bf16)],
    )
    loss, count, norm, grad1, grad2, w1, w2, l1, r1, l2, r2, m1, v1, nb1, m2, v2, nb2 = outs
    return (
        loss.reshape(()), count.reshape(()), norm.reshape(()), grad1.T, grad2.T, w1.T, w2.T,
        l1, r1.T, l2, r2, m1.reshape(width), v1.reshape(width), nb1.reshape(width),
        m2.reshape(classes), v2.reshape(classes), nb2.reshape(classes),
    )


def general_device(
    features, neighbors, label_mask, labels, w_first, w_second, b_first, b_second, l_first, r_first,
    l_second, r_second, l_first_root, r_first_root, l_second_root, r_second_root, m_first, v_first,
    m_second, v_second,
):
    fan_in, width = w_first.shape
    classes = w_second.shape[1]
    scale_in = 1.0 / (neighbors.shape[1] + 1)
    packed = jnp.concatenate([w_first, b_first[None, :], w_second.T], axis=0).astype(bf16)
    packed = lax.all_gather(packed, AXES, axis=1, tiled=True)
    first_full, bias_full, second_full = packed[:fan_in], packed[fan_in], packed[fan_in + 1 :]
    loss = jnp.zeros((), f32)
    grads = jnp.zeros(packed.shape, f32)
    gb2 = jnp.zeros_like(b_second)
    for b in range(features.shape[0] // BLOCK):
        at = slice(b * BLOCK, (b + 1) * BLOCK)
        columns = jnp.arange(BLOCK, dtype=jnp.int32)
        counts = jnp.sum(
            (neighbors[at][:, :, None] == columns[None, None, :]).astype(f32), axis=1
        )
        eye = jnp.eye(BLOCK, dtype=f32)
        matrix = (counts + eye * (2.0 + jnp.sum(counts * eye, axis=1))[:, None]).astype(bf16)
        pooled = (mm(matrix, features[at]) * scale_in).astype(bf16)
        pre = mm(pooled, first_full) + bias_full.astype(f32)
        hidden = jax.nn.gelu(pre).astype(bf16)
        logits = (
            jnp.dot(matrix.astype(f32), mm(hidden, second_full, NT), precision=highest) * scale_in
            + b_second
        )
        log_prob = jax.nn.log_softmax(logits, axis=-1)
        onehot = (labels[at][:, None] == jnp.arange(classes, dtype=jnp.int32)[None, :]).astype(f32)
        weight = label_mask[at].astype(f32)
        loss = loss - jnp.sum(jnp.sum(log_prob * onehot, axis=-1) * weight)
        grad = ((jnp.exp(log_prob) - onehot) * weight[:, None]).astype(bf16)
        gb2 = gb2 + jnp.sum(grad.astype(f32), axis=0)
        back = (mm(matrix, grad, TN) * scale_in).astype(bf16)
        grad_pre = jax.vjp(jax.nn.gelu, pre)[1](mm(back, second_full))[0].astype(bf16)
        grads = grads + jnp.concatenate(
            [
                mm(pooled, grad_pre, TN),
                jnp.sum(grad_pre.astype(f32), axis=0, keepdims=True),
                mm(back, hidden, TN),
            ],
            axis=0,
        )
    count = jnp.sum(label_mask).astype(f32)
    grads, gb2, loss, count = lax.psum((grads, gb2, loss, count), AXES)
    inv = 1.0 / jnp.maximum(count, 1.0)
    grads, gb2 = grads * inv, gb2 * inv
    norm = jnp.sqrt(jnp.sum(grads * grads) + jnp.sum(gb2 * gb2))
    factor = jnp.minimum(1.0, clip_limit / (norm + 1e-06))
    grads, gb2 = grads * factor, gb2 * factor
    at = lax.axis_index(AXES) * width
    own = lax.dynamic_slice_in_dim(grads, at, width, axis=1)
    full_one, full_two = grads[:fan_in], grads[fan_in + 1 :].T
    own_one, own_bias, own_two = own[:fan_in], own[fan_in], own[fan_in + 1 :].T
    dot = functools.partial(jnp.dot, precision=highest)
    keep, add = beta_stat, 1.0 - beta_stat
    m1, v1, b1 = adam_step(b_first, own_bias, m_first, v_first)
    m2, v2, b2 = adam_step(b_second, gb2, m_second, v_second)
    return (
        loss, count, norm, own_one, own_two,
        w_first - rate_first * dot(l_first_root, dot(full_one, r_first_root)),
        w_second - rate_second * dot(dot(l_second_root, full_two), r_second_root),
        keep * l_first + add * dot(full_one, full_one.T),
        keep * r_first + add * dot(full_one.T, own_one),
        keep * l_second + add * dot(own_two, full_two.T),
        keep * r_second + add * dot(full_two.T, full_two),
        m1, v1, b1, m2, v2, b2,
    )


def solution(mesh):
    split0 = P(AXES)
    rows = P(AXES, None)
    columns = P(None, AXES)
    whole = P()
    fast = mesh.shape["dp"] == 16 and mesh.shape["shard"] == 2

    def per_device(*args):
        width = args[4].shape[1]
        return (fast_device if fast and 2 * width == LANES else general_device)(*args)

    return jax.shard_map(
        per_device,
        mesh=mesh,
        in_specs=(
            rows, rows, split0, split0, columns, rows, split0, whole, whole, columns, rows, whole,
            whole, columns, rows, whole, split0, split0, whole, whole,
        ),
        out_specs=(
            whole, whole, whole, columns, rows, columns, rows, whole, columns, rows, whole,
            split0, split0, split0, whole, whole, whole,
        ),
        check_vma=False,
    )
```

```python
import functools

import jax
import jax.numpy as jnp
from jax import lax
from jax.experimental import pallas as pl
from jax.experimental.pallas import tpu as pltpu
from jax.sharding import PartitionSpec as P

STEP = 10
BLOCK = 1024
AXES = ("dp", "shard")

clip_limit = 0.05
beta_stat = 0.95
beta_one = 0.9
beta_two = 0.999
adam_eps = 1e-08
decay_rate = 0.01
rate_bias = 0.2
rate_first = 1000.0
rate_second = 300.0
highest = lax.Precision.HIGHEST

f32 = jnp.float32
bf16 = jnp.bfloat16
NN = (((1,), (0,)), ((), ()))
NT = (((1,), (1,)), ((), ()))
TN = (((0,), (0,)), ((), ()))

ROWS = 160
HALF = 80
TOP = 112
LANES = 128


def mm(a, b, dims=NN):
    return lax.dot_general(a, b, dims, preferred_element_type=f32)


def call(kernel, name, us, limit, out_shape, *args, after=(), scratch=(), **kw):
    n = len(args)

    def body(*refs):
        kernel(*refs[:n], *refs[n + len(after) :])

    kw.setdefault("in_specs", [pl.BlockSpec(memory_space=pltpu.VMEM)] * n)
    kw["in_specs"] = list(kw["in_specs"]) + [pl.BlockSpec(memory_space=pl.ANY)] * len(after)
    return pl.pallas_call(
        body,
        out_shape=out_shape,
        scratch_shapes=scratch,
        compiler_params=pltpu.CompilerParams(vmem_limit_bytes=limit * 2**20),
        cost_estimate=pl.CostEstimate(
            flops=int(us * 1e9), bytes_accessed=int(us * 2e6), transcendentals=0
        ),
        name=name,
        **kw,
    )(*args, *after)


def adam_step(param, grad, first, second):
    first_new = beta_one * first + (1.0 - beta_one) * grad
    second_new = beta_two * second + (1.0 - beta_two) * grad * grad
    corr_one = 1.0 - beta_one**STEP
    corr_two = 1.0 - beta_two**STEP
    update = (
        first_new / corr_one / (jnp.sqrt(second_new / corr_two) + adam_eps) + decay_rate * param
    )
    return (first_new, second_new, param - rate_bias * update)


def pack_kernel(w1t_hbm, w2t_hbm, b_hbm, out_ref, w1t_ref, w2t_ref, b_ref, bottom, sem):
    copies = [
        pltpu.make_async_copy(source, target, sem.at[k])
        for k, (source, target) in enumerate(
            ((w1t_hbm, w1t_ref), (w2t_hbm, w2t_ref), (b_hbm, b_ref))
        )
    ]
    for copy in copies:
        copy.start()
    for copy in copies:
        copy.wait()
    fan_in = w1t_ref.shape[1]
    width = w1t_ref.shape[0]
    classes = w2t_ref.shape[0]
    rows = lax.broadcasted_iota(jnp.int32, (TOP, fan_in), 0)
    cols = lax.broadcasted_iota(jnp.int32, (TOP, fan_in), 1)
    eye = (rows == cols).astype(bf16)
    w1 = mm(eye, w1t_ref[...].astype(bf16), NT)
    rows = lax.broadcasted_iota(jnp.int32, (TOP, width), 0)
    w1 = jnp.where(rows == fan_in, b_ref[...], w1)
    out_ref[:, 0:width] = w1[0:HALF].astype(bf16)
    bottom[...] = jnp.zeros_like(bottom)
    bottom[0 : TOP - HALF, :] = w1[HALF:TOP]
    bottom[TOP - HALF : TOP - HALF + classes, :] = w2t_ref[...]
    out_ref[:, width : 2 * width] = bottom[...].astype(bf16)


def graph_kernel(fan_in, block, nbr_ref, feat_ref, m_ref, p_ref, pt_ref):
    classes = nbr_ref.shape[0]
    scale_in = 1.0 / (classes + 1)
    base = lax.broadcasted_iota(jnp.int32, (16, LANES), 0).astype(jnp.int16)
    one = jnp.ones((16, LANES), bf16)
    zero = jnp.zeros((16, LANES), bf16)
    row = lax.broadcasted_iota(jnp.int32, (LANES, LANES), 0)
    col = lax.broadcasted_iota(jnp.int32, (LANES, LANES), 1)
    base_at = block * BLOCK
    for t in range(BLOCK // LANES):
        at = slice(t * LANES, (t + 1) * LANES)
        slots = [
            jnp.broadcast_to(nbr_ref[k : k + 1, base_at + t * LANES : base_at + (t + 1) * LANES], (16, LANES)).astype(jnp.int16)
            for k in range(classes)
        ]
        for u in range(BLOCK // 16):
            here = base + jnp.int16(u * 16)
            terms = [jnp.where(s == here, one, zero) for s in slots]
            while len(terms) > 1:
                terms = [sum(terms[a : a + 2][1:], terms[a]) for a in range(0, len(terms), 2)]
            m_ref[u * 16 : (u + 1) * 16, at] = terms[0]
        square = m_ref[at, at].astype(f32)
        m_ref[at, at] = jnp.where(row == col, 2.0 * square + 2.0, square).astype(bf16)
    pooled = mm(feat_ref[:, base_at : base_at + BLOCK], m_ref[...]) * scale_in
    rest = LANES - fan_in - 1
    pooled = jnp.concatenate(
        [pooled, jnp.ones((1, BLOCK), f32), jnp.zeros((rest, BLOCK), f32)], axis=0
    )
    pt_ref[...] = pooled[0:TOP].astype(bf16)
    p_ref[...] = pooled.T.astype(bf16)


def forward_kernel(nblk, count, *refs):
    own_refs, other_refs = refs[0:count], refs[count : 2 * count]
    p_refs = refs[2 * count : 2 * count + nblk]
    ww, hid, der, zt, w = refs[2 * count + nblk :]
    group = w.shape[1]
    each = group // LANES // count
    first = lax.axis_index("shard") == 0

    left = lax.broadcasted_iota(jnp.int32, (HALF, LANES), 1) < LANES // 2
    row = lax.broadcasted_iota(jnp.int32, (HALF, LANES), 0)
    for s in range(group // LANES):
        at = slice(s * LANES, (s + 1) * LANES)
        part = slice(s % each * LANES, (s % each + 1) * LANES)
        mine = own_refs[s // each][:, part].astype(f32)
        theirs = other_refs[s // each][:, part].astype(f32)
        lo = jnp.where(first, mine, theirs)
        hi = jnp.where(first, theirs, mine)
        upper = jnp.where(left, lo, pltpu.roll(hi, LANES // 2, 1))
        lower = jnp.where(left, pltpu.roll(lo, LANES // 2, 1), hi)
        w[0:HALF, at] = (0.5 * upper).astype(bf16)
        w[HALF:ROWS, at] = jnp.where(row < TOP - HALF, 0.5 * lower, lower).astype(bf16)
    ww[0:48, :] = w[TOP:ROWS, :]
    ww[48:96, :] = w[TOP:ROWS, :]
    ww[96:128, :] = jnp.zeros((32, group), bf16)

    c0 = 0.7978845608028654
    c1 = c0 * 0.044715
    narrow = 256
    for n in range(group // narrow):
        at = slice(n * narrow, (n + 1) * narrow)
        for b in range(nblk):
            to = slice(b * BLOCK, (b + 1) * BLOCK)
            x = mm(p_refs[b][...], w[0:LANES, at])
            xb = x.astype(bf16)
            k = bf16(8.0 * c1) * (xb * xb)
            s = bf16(1.0) + jnp.tanh(xb * (k + bf16(2.0 * c0)))
            hb = xb * s
            d = s + ((bf16(2.0) - s) * hb) * (bf16(3.0) * k + bf16(2.0 * c0))
            hid[to, at] = hb
            der[to, at] = d.astype(bf16)
            part = mm(w[TOP:ROWS, at], hb, NT)
            zt[b] = part if n == 0 else zt[b] + part


def middle_kernel(nblk, shares, classes, degree, *refs):
    z_refs, refs = refs[0:shares], refs[shares:]
    m_refs, refs = refs[0:nblk], refs[nblk:]
    mask_ref, label_ref, b2_ref, qq, qqt, scal_ref, row_scr = refs
    first = lax.axis_index("shard") == 0
    scale_in = 1.0 / (degree + 1)
    pick = lax.broadcasted_iota(jnp.int32, (48, classes), 0) == lax.broadcasted_iota(
        jnp.int32, (48, classes), 1
    )
    bias = jnp.sum(jnp.where(pick, b2_ref[...], 0.0), axis=1, keepdims=True)
    lane = lax.broadcasted_iota(jnp.int32, (BLOCK, LANES), 1)
    row_scr[...] = jnp.zeros_like(row_scr)
    loss = jnp.zeros((1, 1), f32)
    count = jnp.zeros((1, 1), f32)
    for b in range(nblk):
        zb = sum([z[b] for z in z_refs[1:]], z_refs[0][b])
        z_hi = zb.astype(bf16)
        z_lo = (zb - z_hi.astype(f32)).astype(bf16)
        both = mm(jnp.concatenate([z_hi, z_lo], axis=0), m_refs[b][...])
        logits = (both[0:48] + both[48:96]) * scale_in + bias
        cls = lax.broadcasted_iota(jnp.int32, (48, BLOCK), 0)
        logits = jnp.where(cls < classes, logits, -1e30)
        top = jnp.max(logits, axis=0, keepdims=True)
        e = jnp.exp(logits - top)
        total = jnp.sum(e, axis=0, keepdims=True)
        mine = slice(b * BLOCK, (b + 1) * BLOCK)
        hit = cls == label_ref[mine].reshape(1, BLOCK)
        weight = mask_ref[mine].reshape(1, BLOCK).astype(f32)
        picked = jnp.sum(jnp.where(hit, logits, 0.0), axis=0, keepdims=True)
        loss += jnp.sum((jnp.log(total) + top - picked) * weight, axis=1, keepdims=True)
        count += jnp.sum(weight, axis=1, keepdims=True)
        grad = ((e / total - hit.astype(f32)) * weight).astype(bf16)
        row_scr[:, 0:48] += mm(jnp.ones((8, BLOCK), bf16), grad, NT)
        grad_t = jnp.concatenate([grad.astype(f32), jnp.zeros((80, BLOCK), f32)], axis=0).T
        q = mm(m_refs[b][...], grad_t.astype(bf16)) * scale_in
        q_hi = q.astype(bf16).astype(f32)
        q2 = jnp.where(lane < 48, q_hi, pltpu.roll(q - q_hi, 48, 1))
        qq[b * BLOCK : (b + 1) * BLOCK, :] = (0.5 * q2).astype(bf16)
        qqt[b] = q2.T[0:96].astype(bf16)

    vec = row_scr[0:1, :]
    pos = lax.broadcasted_iota(jnp.int32, vec.shape, 1)
    vec = jnp.where(pos == 48, loss, jnp.where(pos == 49, count, vec))
    part_a = vec.astype(bf16).astype(f32)
    part_b = (vec - part_a).astype(bf16).astype(f32)
    part_c = (vec - part_a - part_b).astype(bf16).astype(f32)
    r16 = lax.broadcasted_iota(jnp.int32, (16, LANES), 0) - jnp.where(first, 5, 8)
    scal_ref[...] = (
        jnp.where(r16 == 0, part_a, 0.0)
        + jnp.where(r16 == 1, part_b, 0.0)
        + jnp.where(r16 == 2, part_c, 0.0)
    )


ORDER = (3, 1, 2)
PASSES = tuple(
    tuple((k, u) for k in range(4) for u in range(4) if (k in ORDER[:2] or u in ORDER[:2]) == early)
    for early in (True, False)
)
PIECES = (ORDER[:2], (0, ORDER[2]))


def lanes_of(first_ref, rest_ref, slots, rows=slice(None)):
    parts = []
    for k, u in slots:
        ref, n = (first_ref, u) if k == 0 else (rest_ref, (k - 1) * 4 + u)
        parts.append(ref[rows, n * LANES : (n + 1) * LANES])
    return jnp.concatenate(parts, axis=1)


def backward_kernel(nblk, slots, *refs):
    qq, qqt = refs[0:2]
    pt_refs = refs[2 : 2 + nblk]
    ww0, hid0, der0, ww1, hid1, der1, scal_ref = refs[2 + nblk : 9 + nblk]
    keep_ref, send_ref = refs[9 + nblk :]
    first = lax.axis_index("shard") == 0
    for n in range(0, len(slots), 4):
        some = slots[n : n + 4]
        wide = len(some) * LANES
        d1 = jnp.zeros((TOP, wide), f32)
        d2 = jnp.zeros((96, wide), f32)
        weights = lanes_of(ww0, ww1, some)
        for b in range(nblk):
            to = slice(b * BLOCK, (b + 1) * BLOCK)
            slope = lanes_of(der0, der1, some, to).astype(f32)
            gp = (mm(qq[to, :], weights) * slope).astype(bf16)
            d1 = d1 + mm(pt_refs[b][...], gp)
            d2 = d2 + mm(qqt[b], lanes_of(hid0, hid1, some, to))
        d2 = d2[0:48] + d2[48:96]
        upper = d1[0:HALF]
        middle = d1[96:TOP]
        if some[0] == (0, 0):
            middle += jnp.concatenate([scal_ref[...], jnp.zeros((16, wide - LANES), f32)], axis=1)
        lower = jnp.concatenate([d1[HALF:96], middle, d2], axis=0)
        at = slice(n * LANES, n * LANES + wide)
        keep_ref[:, at] = jnp.where(first, upper, lower)
        send_ref[:, at] = jnp.where(first, lower, upper)


def turn_kernel(nblk, count, shares, classes, degree, slots, *refs):
    ins, refs = refs[: 2 * count], refs[2 * count :]
    p_refs, refs = refs[:nblk], refs[nblk:]
    pt_refs, refs = refs[:nblk], refs[nblk:]
    early, refs = refs[:4], refs[4:]
    labels, refs = refs[: nblk + 3], refs[nblk + 3 :]
    ww, hid, der, qq, qqt, scal, keep, send, w, zt, row_scr = refs
    forward_kernel(nblk, count, *ins, *p_refs, ww, hid, der, zt, w)
    middle_kernel(nblk, 2, classes, degree, early[3], zt, *labels, qq, qqt, scal, row_scr)
    backward_kernel(
        nblk, slots, qq, qqt, *pt_refs, *early[0:3], ww, hid, der, scal, keep, send
    )


def add_core_kernel(pieces, passes, *refs):
    keeps, gots, outs = refs[0:passes], refs[passes : 2 * passes], refs[2 * passes :]
    first = lax.axis_index("shard") == 0

    def total(slot):
        for p in range(passes):
            if slot in PASSES[p]:
                n = PASSES[p].index(slot)
                at = slice(n * LANES, (n + 1) * LANES)
                return keeps[p][:, at] + gots[p][:, at]
        raise KeyError(slot)

    for k, out in zip(pieces, outs, strict=True):
        for u in range(4):
            picked = jnp.where(first, total((k, u)), total((u, k)))
            out[:, u * LANES : (u + 1) * LANES] = picked.astype(out.dtype)


def add_piece_kernel(own_ref, r1_ref, r2_ref, r3_ref, out_ref):
    out_ref[...] = (
        own_ref[...] + r1_ref[...].astype(f32) + r2_ref[...].astype(f32) + r3_ref[...].astype(f32)
    ).astype(bf16)


def add_line_kernel(h_ref, z1_ref, z2_ref, z3_ref, out_ref):
    for s in range(4):
        here, one, two, three = (
            ref[:, (s ^ k) * LANES : ((s ^ k) + 1) * LANES].astype(f32)
            for k, ref in enumerate((h_ref, z1_ref, z2_ref, z3_ref))
        )
        out_ref[:, s * LANES : (s + 1) * LANES] = ((here + one) + (two + three)).astype(bf16)


def step_kernel(fan_in, classes, *refs):
    own = refs[0:4]
    other = refs[4:8]
    (
        w1t, w2t, b1, b2, l1, r1t, l2, r2, l1_root, r1t_root, l2_root, r2_root, m1, v1, m2, v2,
    ) = refs[8:24]
    (
        loss_o, count_o, norm_o, grad1_o, grad2_o, w1_o, w2_o, l1_o, r1_o, l2_o, r2_o,
        m1_o, v1_o, b1_o, m2_o, v2_o, b2_o,
    ) = refs[24:41]
    g = refs[41]
    chip = lax.axis_index("dp")
    core = lax.axis_index("shard")
    first = core == 0
    half = LANES // 2
    for refs_of, owner in ((own, core), (other, 1 - core)):
        rows = pl.ds(pl.multiple_of(owner * HALF, 16), HALF)
        for k in range(4):
            for u in range(4):
                slot = jnp.where(owner == 0, u * 4 + k, k * 4 + u)
                to = pl.ds(pl.multiple_of((chip ^ slot) * LANES, LANES), LANES)
                g[rows, to] = refs_of[k][:, u * LANES : (u + 1) * LANES]
    mixed = g[96:TOP, :].astype(f32)
    scal = sum(mixed[:, u * LANES : (u + 1) * LANES] for u in range(mixed.shape[1] // LANES))
    keep = lax.broadcasted_iota(jnp.int32, mixed.shape, 0) <= fan_in - 96
    g[96:TOP, :] = jnp.where(keep, mixed, 0.0).astype(bf16)
    row16 = lax.broadcasted_iota(jnp.int32, (16, LANES), 0)
    scal = jnp.where((row16 >= 5) & (row16 <= 10), scal, 0.0)
    vec = jnp.sum(scal, axis=0, keepdims=True)
    pos = lax.broadcasted_iota(jnp.int32, (1, LANES), 1)
    loss = jnp.sum(jnp.where(pos == 48, vec, 0.0), axis=1, keepdims=True)
    count = jnp.sum(jnp.where(pos == 49, vec, 0.0), axis=1, keepdims=True)
    inv = 1.0 / jnp.maximum(count, 1.0)
    gb2 = jnp.where(pos < classes, vec, 0.0) * inv
    whole = g[...]
    stacked = jnp.concatenate(
        [whole, r1t_root[...].astype(bf16), l2_root[...].astype(bf16)], axis=0
    )
    products = mm(stacked, whole, NT)
    gram = products[0:ROWS]
    gi = lax.broadcasted_iota(jnp.int32, gram.shape, 0)
    gj = lax.broadcasted_iota(jnp.int32, gram.shape, 1)
    squares = jnp.sum(jnp.where(gi == gj, gram, 0.0), axis=0, keepdims=True)
    squares = jnp.sum(squares, axis=1, keepdims=True) * inv * inv
    squares = squares + jnp.sum(gb2 * gb2, axis=1, keepdims=True)
    norm = jnp.sqrt(squares)
    factor = jnp.minimum(1.0, clip_limit / (norm + 1e-06))
    s = factor * inv
    ss = (1.0 - beta_stat) * s * s
    loss_o[...] = loss
    count_o[...] = count
    norm_o[...] = norm
    l1_o[...] = beta_stat * l1[...] + ss * gram[0:fan_in, 0:fan_in]
    gram2 = gram[TOP : TOP + classes, TOP : TOP + classes]
    r2_o[...] = beta_stat * r2[...] + ss * gram2

    mine = g[:, pl.ds(pl.multiple_of(chip * LANES, LANES), LANES)].astype(f32)
    mine = jnp.where(first, mine, pltpu.roll(mine, half, 1))[:, 0:half]
    mine_b = mine.astype(bf16)
    eye = (
        lax.broadcasted_iota(jnp.int32, (half, half), 0)
        == lax.broadcasted_iota(jnp.int32, (half, half), 1)
    ).astype(bf16)
    mine_t = mm(eye, mine_b, NT)
    grad1_o[...] = s * mine_t[:, 0:fan_in]
    grad2_o[...] = s * mine[TOP : TOP + classes, :]
    at = lax.broadcasted_iota(jnp.int32, mine_t.shape, 1)
    owns = jnp.concatenate(
        [jnp.where(at < fan_in, mine_t, 0.0), jnp.where(at >= TOP, mine_t, 0.0)], axis=0
    )
    stats = mm(owns.astype(bf16), whole)
    r1_o[...] = beta_stat * r1t[...] + ss * stats[0:half]
    l2_o[...] = beta_stat * l2[...] + ss * stats[half:LANES]
    t1 = products[ROWS : ROWS + half, 0:fan_in]
    t1 = lax.dot_general(t1, l1_root[...], NT, precision=highest, preferred_element_type=f32)
    w1_o[...] = w1t[...] - (rate_first * s) * t1
    t2 = products[ROWS + half : ROWS + LANES, TOP : TOP + classes]
    t2 = lax.dot_general(
        r2_root[...], t2, (((0,), (1,)), ((), ())), precision=highest, preferred_element_type=f32
    )
    w2_o[...] = w2t[...] - (rate_second * s) * t2
    m1_o[...], v1_o[...], b1_o[...] = adam_step(
        b1[...], s * mine[fan_in : fan_in + 1, :], m1[...], v1[...]
    )
    m2_o[...], v2_o[...], b2_o[...] = adam_step(
        b2[...], factor * gb2[:, 0:classes], m2[...], v2[...]
    )


def later(array, after):
    return lax.optimization_barrier((array, after))[0]


def swap(array, bits, bits_one=None):
    count = lax.axis_size(AXES)
    both = (bits, bits if bits_one is None else bits_one)
    return lax.ppermute(array, AXES, [(i, i ^ both[i % 2]) for i in range(count)])


def fast_device(
    features, neighbors, label_mask, labels, w_first, w_second, b_first, b_second, l_first, r_first,
    l_second, r_second, l_first_root, r_first_root, l_second_root, r_second_root, m_first, v_first,
    m_second, v_second,
):
    fan_in, width = w_first.shape
    classes = w_second.shape[1]
    degree = neighbors.shape[1]
    nblk = features.shape[0] // BLOCK
    hidden = width * lax.axis_size(AXES)
    group = hidden // 4
    shape = jax.ShapeDtypeStruct
    w1t, w2t, b1 = w_first.T, w_second.T, b_first.reshape(1, width)

    piece = call(
        pack_kernel, "pack", 1, 60, shape((HALF, LANES), bf16), w1t, w2t, b1,
        in_specs=[pl.BlockSpec(memory_space=pl.ANY)] * 3,
        scratch=[
            pltpu.VMEM(w1t.shape, f32),
            pltpu.VMEM(w2t.shape, f32),
            pltpu.VMEM(b1.shape, f32),
            pltpu.VMEM((HALF, width), f32),
            pltpu.SemaphoreType.DMA((3,)),
        ],
    )
    nbr_t, feat_t = neighbors.T, features.T

    def graph(b, after=()):
        return call(
            functools.partial(graph_kernel, fan_in, b), "graph", 2.6, 4,
            [shape((BLOCK, BLOCK), bf16), shape((BLOCK, LANES), bf16), shape((TOP, BLOCK), bf16)],
            nbr_t, feat_t, after=after,
        )

    graphs = [graph(0)]
    line = [later(swap(piece, 8 * k), graphs[0][2]) for k in (1, 2, 3)]
    line = jnp.concatenate([piece] + line, axis=1)
    plane = [line] + [swap(line, 2 * k) for k in (1, 2, 3)]
    graphs += [graph(b, [line]) for b in range(1, nblk)]
    ms, ps, pts = ([graph[k] for graph in graphs] for k in range(3))
    partner = [swap(later(line, pts[-1]), 1)]

    nodes = nblk * BLOCK
    def forward_shapes(count):
        wide = count * group
        return [
            shape((LANES, wide), bf16), shape((nodes, wide), bf16), shape((nodes, wide), bf16),
        ]

    logit_share = shape((nblk, 48, BLOCK), f32)
    early = call(
        functools.partial(forward_kernel, nblk, 1), "forward", 1.5, 4,
        forward_shapes(1) + [logit_share], line, partner[0], *ps,
        scratch=[pltpu.VMEM((ROWS, group), bf16)],
    )
    partner += [swap(part, 1) for part in plane[1:]]
    half_pass = [shape((HALF, len(PASSES[0]) * LANES), f32)] * 2
    *late, qq, qqt, scal, keep, send = call(
        functools.partial(turn_kernel, nblk, 3, 2, classes, degree, PASSES[0]), "turn", 9, 8,
        forward_shapes(3)
        + [shape((nodes, LANES), bf16), shape((nblk, 96, BLOCK), bf16), shape((16, LANES), f32)]
        + half_pass,
        *plane[1:], *partner[1:], *ps, *pts, *early, *ms, label_mask, labels,
        b_second.reshape(1, classes),
        scratch=[
            pltpu.VMEM((ROWS, 3 * group), bf16),
            pltpu.VMEM((nblk, 48, BLOCK), f32),
            pltpu.VMEM((8, LANES), f32),
        ],
    )
    keeps, gots, received = [], [], []
    for n, (slots, pieces) in enumerate(zip(PASSES, PIECES, strict=True)):
        if n:
            keep, send = call(
                functools.partial(backward_kernel, nblk, slots), "backward", 0.35 * len(slots), 6,
                [shape((HALF, len(slots) * LANES), f32)] * 2,
                qq, qqt, *pts, *early[0:3], *late, scal,
            )
        keeps.append(keep)
        gots.append(swap(send, 1))
        sums = call(
            functools.partial(add_core_kernel, pieces, n + 1), "add_core", 0.3, 4,
            [shape((HALF, group), f32 if k in (0, ORDER[0]) else bf16) for k in pieces],
            *keeps, *gots,
        )
        for k, part in zip(pieces, sums, strict=True):
            received.append(swap(part, 2 * k, 8 * k) if k else part)
    received = [received[n] for n in (2, 0, 1, 3)]
    mine = call(
        add_piece_kernel, "add_piece", 0.3, 2, shape((HALF, group), bf16), *received
    )
    mine = call(
        add_line_kernel, "add_line", 0.3, 2, shape((HALF, group), bf16),
        mine, *[swap(mine, 8 * k, 2 * k) for k in (1, 2, 3)],
    )
    plane = [mine] + [swap(mine, 2 * k, 8 * k) for k in (1, 2, 3)]
    partner = [swap(part, 1) for part in plane]

    one = shape((1, 1), f32)
    row1, row2 = shape((1, width), f32), shape((1, classes), f32)
    outs = call(
        functools.partial(step_kernel, fan_in, classes), "update", 2.5, 8,
        [
            one, one, one, shape(w1t.shape, f32), shape(w2t.shape, f32), shape(w1t.shape, f32),
            shape(w2t.shape, f32), shape(l_first.shape, f32), shape((width, hidden), f32),
            shape((width, hidden), f32), shape(r_second.shape, f32),
            row1, row1, row1, row2, row2, row2,
        ],
        *plane, *partner,
        w1t, w2t, b1, b_second.reshape(1, classes), l_first, r_first.T, l_second, r_second,
        l_first_root, r_first_root.T, l_second_root, r_second_root,
        m_first.reshape(1, width), v_first.reshape(1, width),
        m_second.reshape(1, classes), v_second.reshape(1, classes),
        scratch=[pltpu.VMEM((ROWS, hidden), bf16)],
    )
    loss, count, norm, grad1, grad2, w1, w2, l1, r1, l2, r2, m1, v1, nb1, m2, v2, nb2 = outs
    return (
        loss.reshape(()), count.reshape(()), norm.reshape(()), grad1.T, grad2.T, w1.T, w2.T,
        l1, r1.T, l2, r2, m1.reshape(width), v1.reshape(width), nb1.reshape(width),
        m2.reshape(classes), v2.reshape(classes), nb2.reshape(classes),
    )


def general_device(
    features, neighbors, label_mask, labels, w_first, w_second, b_first, b_second, l_first, r_first,
    l_second, r_second, l_first_root, r_first_root, l_second_root, r_second_root, m_first, v_first,
    m_second, v_second,
):
    fan_in, width = w_first.shape
    classes = w_second.shape[1]
    scale_in = 1.0 / (neighbors.shape[1] + 1)
    packed = jnp.concatenate([w_first, b_first[None, :], w_second.T], axis=0).astype(bf16)
    packed = lax.all_gather(packed, AXES, axis=1, tiled=True)
    first_full, bias_full, second_full = packed[:fan_in], packed[fan_in], packed[fan_in + 1 :]
    loss = jnp.zeros((), f32)
    grads = jnp.zeros(packed.shape, f32)
    gb2 = jnp.zeros_like(b_second)
    for b in range(features.shape[0] // BLOCK):
        at = slice(b * BLOCK, (b + 1) * BLOCK)
        columns = jnp.arange(BLOCK, dtype=jnp.int32)
        counts = jnp.sum(
            (neighbors[at][:, :, None] == columns[None, None, :]).astype(f32), axis=1
        )
        eye = jnp.eye(BLOCK, dtype=f32)
        matrix = (counts + eye * (2.0 + jnp.sum(counts * eye, axis=1))[:, None]).astype(bf16)
        pooled = (mm(matrix, features[at]) * scale_in).astype(bf16)
        pre = mm(pooled, first_full) + bias_full.astype(f32)
        hidden = jax.nn.gelu(pre).astype(bf16)
        logits = (
            jnp.dot(matrix.astype(f32), mm(hidden, second_full, NT), precision=highest) * scale_in
            + b_second
        )
        log_prob = jax.nn.log_softmax(logits, axis=-1)
        onehot = (labels[at][:, None] == jnp.arange(classes, dtype=jnp.int32)[None, :]).astype(f32)
        weight = label_mask[at].astype(f32)
        loss = loss - jnp.sum(jnp.sum(log_prob * onehot, axis=-1) * weight)
        grad = ((jnp.exp(log_prob) - onehot) * weight[:, None]).astype(bf16)
        gb2 = gb2 + jnp.sum(grad.astype(f32), axis=0)
        back = (mm(matrix, grad, TN) * scale_in).astype(bf16)
        grad_pre = jax.vjp(jax.nn.gelu, pre)[1](mm(back, second_full))[0].astype(bf16)
        grads = grads + jnp.concatenate(
            [
                mm(pooled, grad_pre, TN),
                jnp.sum(grad_pre.astype(f32), axis=0, keepdims=True),
                mm(back, hidden, TN),
            ],
            axis=0,
        )
    count = jnp.sum(label_mask).astype(f32)
    grads, gb2, loss, count = lax.psum((grads, gb2, loss, count), AXES)
    inv = 1.0 / jnp.maximum(count, 1.0)
    grads, gb2 = grads * inv, gb2 * inv
    norm = jnp.sqrt(jnp.sum(grads * grads) + jnp.sum(gb2 * gb2))
    factor = jnp.minimum(1.0, clip_limit / (norm + 1e-06))
    grads, gb2 = grads * factor, gb2 * factor
    at = lax.axis_index(AXES) * width
    own = lax.dynamic_slice_in_dim(grads, at, width, axis=1)
    full_one, full_two = grads[:fan_in], grads[fan_in + 1 :].T
    own_one, own_bias, own_two = own[:fan_in], own[fan_in], own[fan_in + 1 :].T
    dot = functools.partial(jnp.dot, precision=highest)
    keep, add = beta_stat, 1.0 - beta_stat
    m1, v1, b1 = adam_step(b_first, own_bias, m_first, v_first)
    m2, v2, b2 = adam_step(b_second, gb2, m_second, v_second)
    return (
        loss, count, norm, own_one, own_two,
        w_first - rate_first * dot(l_first_root, dot(full_one, r_first_root)),
        w_second - rate_second * dot(dot(l_second_root, full_two), r_second_root),
        keep * l_first + add * dot(full_one, full_one.T),
        keep * r_first + add * dot(full_one.T, own_one),
        keep * l_second + add * dot(own_two, full_two.T),
        keep * r_second + add * dot(full_two.T, full_two),
        m1, v1, b1, m2, v2, b2,
    )


def solution(mesh):
    split0 = P(AXES)
    rows = P(AXES, None)
    columns = P(None, AXES)
    whole = P()
    fast = mesh.shape["dp"] == 16 and mesh.shape["shard"] == 2

    def per_device(*args):
        width = args[4].shape[1]
        return (fast_device if fast and 2 * width == LANES else general_device)(*args)

    return jax.shard_map(
        per_device,
        mesh=mesh,
        in_specs=(
            rows, rows, split0, split0, columns, rows, split0, whole, whole, columns, rows, whole,
            whole, columns, rows, whole, split0, split0, whole, whole,
        ),
        out_specs=(
            whole, whole, whole, columns, rows, columns, rows, whole, columns, rows, whole,
            split0, split0, split0, whole, whole, whole,
        ),
        check_vma=False,
    )
```

```python
import functools

import jax
import jax.numpy as jnp
from jax import lax
from jax.experimental import pallas as pl
from jax.experimental.pallas import tpu as pltpu
from jax.sharding import PartitionSpec as P

STEP = 10
BLOCK = 1024
AXES = ("dp", "shard")

clip_limit = 0.05
beta_stat = 0.95
beta_one = 0.9
beta_two = 0.999
adam_eps = 1e-08
decay_rate = 0.01
rate_bias = 0.2
rate_first = 1000.0
rate_second = 300.0
highest = lax.Precision.HIGHEST

f32 = jnp.float32
bf16 = jnp.bfloat16
NN = (((1,), (0,)), ((), ()))
NT = (((1,), (1,)), ((), ()))
TN = (((0,), (0,)), ((), ()))

ROWS = 160
HALF = 80
TOP = 112
LANES = 128


def mm(a, b, dims=NN):
    return lax.dot_general(a, b, dims, preferred_element_type=f32)


def call(kernel, name, us, limit, out_shape, *args, after=(), scratch=(), **kw):
    n = len(args)

    def body(*refs):
        kernel(*refs[:n], *refs[n + len(after) :])

    kw.setdefault("in_specs", [pl.BlockSpec(memory_space=pltpu.VMEM)] * n)
    kw["in_specs"] = list(kw["in_specs"]) + [pl.BlockSpec(memory_space=pl.ANY)] * len(after)
    return pl.pallas_call(
        body,
        out_shape=out_shape,
        scratch_shapes=scratch,
        compiler_params=pltpu.CompilerParams(vmem_limit_bytes=limit * 2**20),
        cost_estimate=pl.CostEstimate(
            flops=int(us * 1e9), bytes_accessed=int(us * 2e6), transcendentals=0
        ),
        name=name,
        **kw,
    )(*args, *after)


def adam_step(param, grad, first, second):
    first_new = beta_one * first + (1.0 - beta_one) * grad
    second_new = beta_two * second + (1.0 - beta_two) * grad * grad
    corr_one = 1.0 - beta_one**STEP
    corr_two = 1.0 - beta_two**STEP
    update = (
        first_new / corr_one / (jnp.sqrt(second_new / corr_two) + adam_eps) + decay_rate * param
    )
    return (first_new, second_new, param - rate_bias * update)


def pack_kernel(w1t_hbm, w2t_hbm, b_hbm, out_ref, w1t_ref, w2t_ref, b_ref, bottom, sem):
    copies = [
        pltpu.make_async_copy(source, target, sem.at[k])
        for k, (source, target) in enumerate(
            ((w1t_hbm, w1t_ref), (w2t_hbm, w2t_ref), (b_hbm, b_ref))
        )
    ]
    for copy in copies:
        copy.start()
    for copy in copies:
        copy.wait()
    fan_in = w1t_ref.shape[1]
    width = w1t_ref.shape[0]
    classes = w2t_ref.shape[0]
    rows = lax.broadcasted_iota(jnp.int32, (TOP, fan_in), 0)
    cols = lax.broadcasted_iota(jnp.int32, (TOP, fan_in), 1)
    eye = (rows == cols).astype(bf16)
    w1 = mm(eye, w1t_ref[...].astype(bf16), NT)
    rows = lax.broadcasted_iota(jnp.int32, (TOP, width), 0)
    w1 = jnp.where(rows == fan_in, b_ref[...], w1)
    out_ref[:, 0:width] = w1[0:HALF].astype(bf16)
    bottom[...] = jnp.zeros_like(bottom)
    bottom[0 : TOP - HALF, :] = w1[HALF:TOP]
    bottom[TOP - HALF : TOP - HALF + classes, :] = w2t_ref[...]
    out_ref[:, width : 2 * width] = bottom[...].astype(bf16)


def graph_kernel(fan_in, block, nbr_ref, feat_ref, m_ref, p_ref, pt_ref):
    classes = nbr_ref.shape[0]
    scale_in = 1.0 / (classes + 1)
    base = lax.broadcasted_iota(jnp.int32, (16, LANES), 0).astype(jnp.int16)
    one = jnp.ones((16, LANES), bf16)
    zero = jnp.zeros((16, LANES), bf16)
    row = lax.broadcasted_iota(jnp.int32, (LANES, LANES), 0)
    col = lax.broadcasted_iota(jnp.int32, (LANES, LANES), 1)
    base_at = block * BLOCK
    for t in range(BLOCK // LANES):
        at = slice(t * LANES, (t + 1) * LANES)
        slots = [
            jnp.broadcast_to(nbr_ref[k : k + 1, base_at + t * LANES : base_at + (t + 1) * LANES], (16, LANES)).astype(jnp.int16)
            for k in range(classes)
        ]
        for u in range(BLOCK // 16):
            here = base + jnp.int16(u * 16)
            terms = [jnp.where(s == here, one, zero) for s in slots]
            while len(terms) > 1:
                terms = [sum(terms[a : a + 2][1:], terms[a]) for a in range(0, len(terms), 2)]
            m_ref[u * 16 : (u + 1) * 16, at] = terms[0]
        square = m_ref[at, at].astype(f32)
        m_ref[at, at] = jnp.where(row == col, 2.0 * square + 2.0, square).astype(bf16)
    pooled = mm(feat_ref[:, base_at : base_at + BLOCK], m_ref[...]) * scale_in
    rest = LANES - fan_in - 1
    pooled = jnp.concatenate(
        [pooled, jnp.ones((1, BLOCK), f32), jnp.zeros((rest, BLOCK), f32)], axis=0
    )
    pt_ref[...] = pooled[0:TOP].astype(bf16)
    p_ref[...] = pooled.T.astype(bf16)


def forward_kernel(nblk, count, *refs):
    own_refs, other_refs = refs[0:count], refs[count : 2 * count]
    p_refs = refs[2 * count : 2 * count + nblk]
    ww, hid, der, zt, w = refs[2 * count + nblk :]
    group = w.shape[1]
    each = group // LANES // count
    first = lax.axis_index("shard") == 0

    left = lax.broadcasted_iota(jnp.int32, (HALF, LANES), 1) < LANES // 2
    row = lax.broadcasted_iota(jnp.int32, (HALF, LANES), 0)
    for s in range(group // LANES):
        at = slice(s * LANES, (s + 1) * LANES)
        part = slice(s % each * LANES, (s % each + 1) * LANES)
        mine = own_refs[s // each][:, part].astype(f32)
        theirs = other_refs[s // each][:, part].astype(f32)
        lo = jnp.where(first, mine, theirs)
        hi = jnp.where(first, theirs, mine)
        upper = jnp.where(left, lo, pltpu.roll(hi, LANES // 2, 1))
        lower = jnp.where(left, pltpu.roll(lo, LANES // 2, 1), hi)
        w[0:HALF, at] = (0.5 * upper).astype(bf16)
        w[HALF:ROWS, at] = jnp.where(row < TOP - HALF, 0.5 * lower, lower).astype(bf16)
    ww[0:48, :] = w[TOP:ROWS, :]
    ww[48:96, :] = w[TOP:ROWS, :]
    ww[96:128, :] = jnp.zeros((32, group), bf16)

    c0 = 0.7978845608028654
    c1 = c0 * 0.044715
    narrow = 256
    for n in range(group // narrow):
        at = slice(n * narrow, (n + 1) * narrow)
        for b in range(nblk):
            to = slice(b * BLOCK, (b + 1) * BLOCK)
            x = mm(p_refs[b][...], w[0:LANES, at])
            xb = x.astype(bf16)
            k = bf16(8.0 * c1) * (xb * xb)
            s = bf16(1.0) + jnp.tanh(xb * (k + bf16(2.0 * c0)))
            hb = xb * s
            d = s + ((bf16(2.0) - s) * hb) * (bf16(3.0) * k + bf16(2.0 * c0))
            hid[to, at] = hb
            der[to, at] = d.astype(bf16)
            part = mm(w[TOP:ROWS, at], hb, NT)
            zt[b] = part if n == 0 else zt[b] + part


def middle_kernel(nblk, shares, classes, degree, *refs):
    z_refs, refs = refs[0:shares], refs[shares:]
    m_refs, refs = refs[0:nblk], refs[nblk:]
    mask_ref, label_ref, b2_ref, qq, qqt, scal_ref, row_scr = refs
    first = lax.axis_index("shard") == 0
    scale_in = 1.0 / (degree + 1)
    pick = lax.broadcasted_iota(jnp.int32, (48, classes), 0) == lax.broadcasted_iota(
        jnp.int32, (48, classes), 1
    )
    bias = jnp.sum(jnp.where(pick, b2_ref[...], 0.0), axis=1, keepdims=True)
    lane = lax.broadcasted_iota(jnp.int32, (BLOCK, LANES), 1)
    row_scr[...] = jnp.zeros_like(row_scr)
    loss = jnp.zeros((1, 1), f32)
    count = jnp.zeros((1, 1), f32)
    for b in range(nblk):
        zb = sum([z[b] for z in z_refs[1:]], z_refs[0][b])
        z_hi = zb.astype(bf16)
        z_lo = (zb - z_hi.astype(f32)).astype(bf16)
        both = mm(jnp.concatenate([z_hi, z_lo], axis=0), m_refs[b][...])
        logits = (both[0:48] + both[48:96]) * scale_in + bias
        cls = lax.broadcasted_iota(jnp.int32, (48, BLOCK), 0)
        logits = jnp.where(cls < classes, logits, -1e30)
        top = jnp.max(logits, axis=0, keepdims=True)
        e = jnp.exp(logits - top)
        total = jnp.sum(e, axis=0, keepdims=True)
        mine = slice(b * BLOCK, (b + 1) * BLOCK)
        hit = cls == label_ref[mine].reshape(1, BLOCK)
        weight = mask_ref[mine].reshape(1, BLOCK).astype(f32)
        picked = jnp.sum(jnp.where(hit, logits, 0.0), axis=0, keepdims=True)
        loss += jnp.sum((jnp.log(total) + top - picked) * weight, axis=1, keepdims=True)
        count += jnp.sum(weight, axis=1, keepdims=True)
        grad = ((e / total - hit.astype(f32)) * weight).astype(bf16)
        row_scr[:, 0:48] += mm(jnp.ones((8, BLOCK), bf16), grad, NT)
        grad_t = jnp.concatenate([grad.astype(f32), jnp.zeros((80, BLOCK), f32)], axis=0).T
        q = mm(m_refs[b][...], grad_t.astype(bf16)) * scale_in
        q_hi = q.astype(bf16).astype(f32)
        q2 = jnp.where(lane < 48, q_hi, pltpu.roll(q - q_hi, 48, 1))
        qq[b * BLOCK : (b + 1) * BLOCK, :] = (0.5 * q2).astype(bf16)
        qqt[b] = q2.T[0:96].astype(bf16)

    vec = row_scr[0:1, :]
    pos = lax.broadcasted_iota(jnp.int32, vec.shape, 1)
    vec = jnp.where(pos == 48, loss, jnp.where(pos == 49, count, vec))
    part_a = vec.astype(bf16).astype(f32)
    part_b = (vec - part_a).astype(bf16).astype(f32)
    part_c = (vec - part_a - part_b).astype(bf16).astype(f32)
    r16 = lax.broadcasted_iota(jnp.int32, (16, LANES), 0) - jnp.where(first, 5, 8)
    scal_ref[...] = (
        jnp.where(r16 == 0, part_a, 0.0)
        + jnp.where(r16 == 1, part_b, 0.0)
        + jnp.where(r16 == 2, part_c, 0.0)
    )


ORDER = (3, 1, 2)
PASSES = tuple(
    tuple((k, u) for k in range(4) for u in range(4) if (k in ORDER[:2] or u in ORDER[:2]) == early)
    for early in (True, False)
)
PIECES = (ORDER[:2], (0, ORDER[2]))


def lanes_of(first_ref, rest_ref, slots, rows=slice(None)):
    parts = []
    for k, u in slots:
        ref, n = (first_ref, u) if k == 0 else (rest_ref, (k - 1) * 4 + u)
        parts.append(ref[rows, n * LANES : (n + 1) * LANES])
    return jnp.concatenate(parts, axis=1)


def backward_kernel(nblk, slots, *refs):
    qq, qqt = refs[0:2]
    pt_refs = refs[2 : 2 + nblk]
    ww0, hid0, der0, ww1, hid1, der1, scal_ref = refs[2 + nblk : 9 + nblk]
    keep_ref, send_ref = refs[9 + nblk :]
    first = lax.axis_index("shard") == 0
    for n in range(0, len(slots), 4):
        some = slots[n : n + 4]
        wide = len(some) * LANES
        d1 = jnp.zeros((TOP, wide), f32)
        d2 = jnp.zeros((96, wide), f32)
        weights = lanes_of(ww0, ww1, some)
        for b in range(nblk):
            to = slice(b * BLOCK, (b + 1) * BLOCK)
            slope = lanes_of(der0, der1, some, to).astype(f32)
            gp = (mm(qq[to, :], weights) * slope).astype(bf16)
            d1 = d1 + mm(pt_refs[b][...], gp)
            d2 = d2 + mm(qqt[b], lanes_of(hid0, hid1, some, to))
        d2 = d2[0:48] + d2[48:96]
        upper = d1[0:HALF]
        middle = d1[96:TOP]
        if some[0] == (0, 0):
            middle += jnp.concatenate([scal_ref[...], jnp.zeros((16, wide - LANES), f32)], axis=1)
        lower = jnp.concatenate([d1[HALF:96], middle, d2], axis=0)
        at = slice(n * LANES, n * LANES + wide)
        keep_ref[:, at] = jnp.where(first, upper, lower)
        send_ref[:, at] = jnp.where(first, lower, upper)


def turn_kernel(nblk, count, shares, classes, degree, slots, *refs):
    ins, refs = refs[: 2 * count], refs[2 * count :]
    p_refs, refs = refs[:nblk], refs[nblk:]
    pt_refs, refs = refs[:nblk], refs[nblk:]
    early, refs = refs[:4], refs[4:]
    labels, refs = refs[: nblk + 3], refs[nblk + 3 :]
    ww, hid, der, qq, qqt, scal, keep, send, w, zt, row_scr = refs
    forward_kernel(nblk, count, *ins, *p_refs, ww, hid, der, zt, w)
    middle_kernel(nblk, 2, classes, degree, early[3], zt, *labels, qq, qqt, scal, row_scr)
    backward_kernel(
        nblk, slots, qq, qqt, *pt_refs, *early[0:3], ww, hid, der, scal, keep, send
    )


def add_core_kernel(pieces, passes, *refs):
    keeps, gots, outs = refs[0:passes], refs[passes : 2 * passes], refs[2 * passes :]
    first = lax.axis_index("shard") == 0

    def total(slot):
        for p in range(passes):
            if slot in PASSES[p]:
                n = PASSES[p].index(slot)
                at = slice(n * LANES, (n + 1) * LANES)
                return keeps[p][:, at] + gots[p][:, at]
        raise KeyError(slot)

    for k, out in zip(pieces, outs, strict=True):
        for u in range(4):
            picked = jnp.where(first, total((k, u)), total((u, k)))
            out[:, u * LANES : (u + 1) * LANES] = picked.astype(out.dtype)


def add_first_kernel(own_ref, got_ref, out_ref):
    out_ref[...] = own_ref[...] + got_ref[...].astype(f32)


def add_piece_kernel(own_ref, one_ref, two_ref, out_ref):
    out_ref[...] = (own_ref[...] + one_ref[...].astype(f32) + two_ref[...].astype(f32)).astype(bf16)


def add_line_kernel(h_ref, z1_ref, z2_ref, z3_ref, out_ref):
    for s in range(4):
        here, one, two, three = (
            ref[:, (s ^ k) * LANES : ((s ^ k) + 1) * LANES].astype(f32)
            for k, ref in enumerate((h_ref, z1_ref, z2_ref, z3_ref))
        )
        out_ref[:, s * LANES : (s + 1) * LANES] = ((here + one) + (two + three)).astype(bf16)


def step_kernel(fan_in, classes, *refs):
    own = refs[0:4]
    other = refs[4:8]
    (
        w1t, w2t, b1, b2, l1, r1t, l2, r2, l1_root, r1t_root, l2_root, r2_root, m1, v1, m2, v2,
    ) = refs[8:24]
    (
        loss_o, count_o, norm_o, grad1_o, grad2_o, w1_o, w2_o, l1_o, r1_o, l2_o, r2_o,
        m1_o, v1_o, b1_o, m2_o, v2_o, b2_o,
    ) = refs[24:41]
    g = refs[41]
    chip = lax.axis_index("dp")
    core = lax.axis_index("shard")
    first = core == 0
    half = LANES // 2
    for refs_of, owner in ((own, core), (other, 1 - core)):
        rows = pl.ds(pl.multiple_of(owner * HALF, 16), HALF)
        for k in range(4):
            for u in range(4):
                slot = jnp.where(owner == 0, u * 4 + k, k * 4 + u)
                to = pl.ds(pl.multiple_of((chip ^ slot) * LANES, LANES), LANES)
                g[rows, to] = refs_of[k][:, u * LANES : (u + 1) * LANES]
    mixed = g[96:TOP, :].astype(f32)
    scal = sum(mixed[:, u * LANES : (u + 1) * LANES] for u in range(mixed.shape[1] // LANES))
    keep = lax.broadcasted_iota(jnp.int32, mixed.shape, 0) <= fan_in - 96
    g[96:TOP, :] = jnp.where(keep, mixed, 0.0).astype(bf16)
    row16 = lax.broadcasted_iota(jnp.int32, (16, LANES), 0)
    scal = jnp.where((row16 >= 5) & (row16 <= 10), scal, 0.0)
    vec = jnp.sum(scal, axis=0, keepdims=True)
    pos = lax.broadcasted_iota(jnp.int32, (1, LANES), 1)
    loss = jnp.sum(jnp.where(pos == 48, vec, 0.0), axis=1, keepdims=True)
    count = jnp.sum(jnp.where(pos == 49, vec, 0.0), axis=1, keepdims=True)
    inv = 1.0 / jnp.maximum(count, 1.0)
    gb2 = jnp.where(pos < classes, vec, 0.0) * inv
    whole = g[...]
    stacked = jnp.concatenate(
        [whole, r1t_root[...].astype(bf16), l2_root[...].astype(bf16)], axis=0
    )
    products = mm(stacked, whole, NT)
    gram = products[0:ROWS]
    gi = lax.broadcasted_iota(jnp.int32, gram.shape, 0)
    gj = lax.broadcasted_iota(jnp.int32, gram.shape, 1)
    squares = jnp.sum(jnp.where(gi == gj, gram, 0.0), axis=0, keepdims=True)
    squares = jnp.sum(squares, axis=1, keepdims=True) * inv * inv
    squares = squares + jnp.sum(gb2 * gb2, axis=1, keepdims=True)
    norm = jnp.sqrt(squares)
    factor = jnp.minimum(1.0, clip_limit / (norm + 1e-06))
    s = factor * inv
    ss = (1.0 - beta_stat) * s * s
    loss_o[...] = loss
    count_o[...] = count
    norm_o[...] = norm
    l1_o[...] = beta_stat * l1[...] + ss * gram[0:fan_in, 0:fan_in]
    gram2 = gram[TOP : TOP + classes, TOP : TOP + classes]
    r2_o[...] = beta_stat * r2[...] + ss * gram2

    mine = g[:, pl.ds(pl.multiple_of(chip * LANES, LANES), LANES)].astype(f32)
    mine = jnp.where(first, mine, pltpu.roll(mine, half, 1))[:, 0:half]
    mine_b = mine.astype(bf16)
    eye = (
        lax.broadcasted_iota(jnp.int32, (half, half), 0)
        == lax.broadcasted_iota(jnp.int32, (half, half), 1)
    ).astype(bf16)
    mine_t = mm(eye, mine_b, NT)
    grad1_o[...] = s * mine_t[:, 0:fan_in]
    grad2_o[...] = s * mine[TOP : TOP + classes, :]
    at = lax.broadcasted_iota(jnp.int32, mine_t.shape, 1)
    owns = jnp.concatenate(
        [jnp.where(at < fan_in, mine_t, 0.0), jnp.where(at >= TOP, mine_t, 0.0)], axis=0
    )
    stats = mm(owns.astype(bf16), whole)
    r1_o[...] = beta_stat * r1t[...] + ss * stats[0:half]
    l2_o[...] = beta_stat * l2[...] + ss * stats[half:LANES]
    t1 = products[ROWS : ROWS + half, 0:fan_in]
    t1 = lax.dot_general(t1, l1_root[...], NT, precision=highest, preferred_element_type=f32)
    w1_o[...] = w1t[...] - (rate_first * s) * t1
    t2 = products[ROWS + half : ROWS + LANES, TOP : TOP + classes]
    t2 = lax.dot_general(
        r2_root[...], t2, (((0,), (1,)), ((), ())), precision=highest, preferred_element_type=f32
    )
    w2_o[...] = w2t[...] - (rate_second * s) * t2
    m1_o[...], v1_o[...], b1_o[...] = adam_step(
        b1[...], s * mine[fan_in : fan_in + 1, :], m1[...], v1[...]
    )
    m2_o[...], v2_o[...], b2_o[...] = adam_step(
        b2[...], factor * gb2[:, 0:classes], m2[...], v2[...]
    )


def later(array, after):
    return lax.optimization_barrier((array, after))[0]


def swap(array, bits, bits_one=None):
    count = lax.axis_size(AXES)
    both = (bits, bits if bits_one is None else bits_one)
    return lax.ppermute(array, AXES, [(i, i ^ both[i % 2]) for i in range(count)])


def fast_device(
    features, neighbors, label_mask, labels, w_first, w_second, b_first, b_second, l_first, r_first,
    l_second, r_second, l_first_root, r_first_root, l_second_root, r_second_root, m_first, v_first,
    m_second, v_second,
):
    fan_in, width = w_first.shape
    classes = w_second.shape[1]
    degree = neighbors.shape[1]
    nblk = features.shape[0] // BLOCK
    hidden = width * lax.axis_size(AXES)
    group = hidden // 4
    shape = jax.ShapeDtypeStruct
    w1t, w2t, b1 = w_first.T, w_second.T, b_first.reshape(1, width)

    piece = call(
        pack_kernel, "pack", 1, 60, shape((HALF, LANES), bf16), w1t, w2t, b1,
        in_specs=[pl.BlockSpec(memory_space=pl.ANY)] * 3,
        scratch=[
            pltpu.VMEM(w1t.shape, f32),
            pltpu.VMEM(w2t.shape, f32),
            pltpu.VMEM(b1.shape, f32),
            pltpu.VMEM((HALF, width), f32),
            pltpu.SemaphoreType.DMA((3,)),
        ],
    )
    nbr_t, feat_t = neighbors.T, features.T

    def graph(b, after=()):
        return call(
            functools.partial(graph_kernel, fan_in, b), "graph", 2.6, 4,
            [shape((BLOCK, BLOCK), bf16), shape((BLOCK, LANES), bf16), shape((TOP, BLOCK), bf16)],
            nbr_t, feat_t, after=after,
        )

    graphs = [graph(0)]
    line = [later(swap(piece, 8 * k), graphs[0][2]) for k in (1, 2, 3)]
    line = jnp.concatenate([piece] + line, axis=1)
    plane = [line] + [swap(line, 2 * k) for k in (1, 2, 3)]
    graphs += [graph(b, [line]) for b in range(1, nblk)]
    ms, ps, pts = ([graph[k] for graph in graphs] for k in range(3))
    partner = [swap(later(line, pts[-1]), 1)]

    nodes = nblk * BLOCK
    def forward_shapes(count):
        wide = count * group
        return [
            shape((LANES, wide), bf16), shape((nodes, wide), bf16), shape((nodes, wide), bf16),
        ]

    logit_share = shape((nblk, 48, BLOCK), f32)
    early = call(
        functools.partial(forward_kernel, nblk, 1), "forward", 1.5, 4,
        forward_shapes(1) + [logit_share], line, partner[0], *ps,
        scratch=[pltpu.VMEM((ROWS, group), bf16)],
    )
    partner += [swap(part, 1) for part in plane[1:]]
    half_pass = [shape((HALF, len(PASSES[0]) * LANES), f32)] * 2
    *late, qq, qqt, scal, keep, send = call(
        functools.partial(turn_kernel, nblk, 3, 2, classes, degree, PASSES[0]), "turn", 9, 8,
        forward_shapes(3)
        + [shape((nodes, LANES), bf16), shape((nblk, 96, BLOCK), bf16), shape((16, LANES), f32)]
        + half_pass,
        *plane[1:], *partner[1:], *ps, *pts, *early, *ms, label_mask, labels,
        b_second.reshape(1, classes),
        scratch=[
            pltpu.VMEM((ROWS, 3 * group), bf16),
            pltpu.VMEM((nblk, 48, BLOCK), f32),
            pltpu.VMEM((8, LANES), f32),
        ],
    )
    keeps, gots, received = [], [], []
    for n, (slots, pieces) in enumerate(zip(PASSES, PIECES, strict=True)):
        if n:
            keep, send = call(
                functools.partial(backward_kernel, nblk, slots), "backward", 0.35 * len(slots), 6,
                [shape((HALF, len(slots) * LANES), f32)] * 2,
                qq, qqt, *pts, *early[0:3], *late, scal,
            )
        keeps.append(keep)
        gots.append(swap(send, 1))
        sums = call(
            functools.partial(add_core_kernel, pieces, n + 1), "add_core", 0.3, 4,
            [shape((HALF, group), bf16 if k else f32) for k in pieces],
            *keeps, *gots,
        )
        for k, part in zip(pieces, sums, strict=True):
            received.append(swap(part, 2 * k, 8 * k) if k else part)
    mine = call(
        add_first_kernel, "add_first", 1, 2, shape((HALF, group), f32), received[2], received[0]
    )
    mine = call(
        add_piece_kernel, "add_piece", 0.3, 2, shape((HALF, group), bf16),
        mine, received[1], received[3],
    )
    mine = call(
        add_line_kernel, "add_line", 0.3, 2, shape((HALF, group), bf16),
        mine, *[swap(mine, 8 * k, 2 * k) for k in (1, 2, 3)],
    )
    plane = [mine] + [swap(mine, 2 * k, 8 * k) for k in (1, 2, 3)]
    partner = [swap(part, 1) for part in plane]

    one = shape((1, 1), f32)
    row1, row2 = shape((1, width), f32), shape((1, classes), f32)
    outs = call(
        functools.partial(step_kernel, fan_in, classes), "update", 2.5, 8,
        [
            one, one, one, shape(w1t.shape, f32), shape(w2t.shape, f32), shape(w1t.shape, f32),
            shape(w2t.shape, f32), shape(l_first.shape, f32), shape((width, hidden), f32),
            shape((width, hidden), f32), shape(r_second.shape, f32),
            row1, row1, row1, row2, row2, row2,
        ],
        *plane, *partner,
        w1t, w2t, b1, b_second.reshape(1, classes), l_first, r_first.T, l_second, r_second,
        l_first_root, r_first_root.T, l_second_root, r_second_root,
        m_first.reshape(1, width), v_first.reshape(1, width),
        m_second.reshape(1, classes), v_second.reshape(1, classes),
        scratch=[pltpu.VMEM((ROWS, hidden), bf16)],
    )
    loss, count, norm, grad1, grad2, w1, w2, l1, r1, l2, r2, m1, v1, nb1, m2, v2, nb2 = outs
    return (
        loss.reshape(()), count.reshape(()), norm.reshape(()), grad1.T, grad2.T, w1.T, w2.T,
        l1, r1.T, l2, r2, m1.reshape(width), v1.reshape(width), nb1.reshape(width),
        m2.reshape(classes), v2.reshape(classes), nb2.reshape(classes),
    )


def general_device(
    features, neighbors, label_mask, labels, w_first, w_second, b_first, b_second, l_first, r_first,
    l_second, r_second, l_first_root, r_first_root, l_second_root, r_second_root, m_first, v_first,
    m_second, v_second,
):
    fan_in, width = w_first.shape
    classes = w_second.shape[1]
    scale_in = 1.0 / (neighbors.shape[1] + 1)
    packed = jnp.concatenate([w_first, b_first[None, :], w_second.T], axis=0).astype(bf16)
    packed = lax.all_gather(packed, AXES, axis=1, tiled=True)
    first_full, bias_full, second_full = packed[:fan_in], packed[fan_in], packed[fan_in + 1 :]
    loss = jnp.zeros((), f32)
    grads = jnp.zeros(packed.shape, f32)
    gb2 = jnp.zeros_like(b_second)
    for b in range(features.shape[0] // BLOCK):
        at = slice(b * BLOCK, (b + 1) * BLOCK)
        columns = jnp.arange(BLOCK, dtype=jnp.int32)
        counts = jnp.sum(
            (neighbors[at][:, :, None] == columns[None, None, :]).astype(f32), axis=1
        )
        eye = jnp.eye(BLOCK, dtype=f32)
        matrix = (counts + eye * (2.0 + jnp.sum(counts * eye, axis=1))[:, None]).astype(bf16)
        pooled = (mm(matrix, features[at]) * scale_in).astype(bf16)
        pre = mm(pooled, first_full) + bias_full.astype(f32)
        hidden = jax.nn.gelu(pre).astype(bf16)
        logits = (
            jnp.dot(matrix.astype(f32), mm(hidden, second_full, NT), precision=highest) * scale_in
            + b_second
        )
        log_prob = jax.nn.log_softmax(logits, axis=-1)
        onehot = (labels[at][:, None] == jnp.arange(classes, dtype=jnp.int32)[None, :]).astype(f32)
        weight = label_mask[at].astype(f32)
        loss = loss - jnp.sum(jnp.sum(log_prob * onehot, axis=-1) * weight)
        grad = ((jnp.exp(log_prob) - onehot) * weight[:, None]).astype(bf16)
        gb2 = gb2 + jnp.sum(grad.astype(f32), axis=0)
        back = (mm(matrix, grad, TN) * scale_in).astype(bf16)
        grad_pre = jax.vjp(jax.nn.gelu, pre)[1](mm(back, second_full))[0].astype(bf16)
        grads = grads + jnp.concatenate(
            [
                mm(pooled, grad_pre, TN),
                jnp.sum(grad_pre.astype(f32), axis=0, keepdims=True),
                mm(back, hidden, TN),
            ],
            axis=0,
        )
    count = jnp.sum(label_mask).astype(f32)
    grads, gb2, loss, count = lax.psum((grads, gb2, loss, count), AXES)
    inv = 1.0 / jnp.maximum(count, 1.0)
    grads, gb2 = grads * inv, gb2 * inv
    norm = jnp.sqrt(jnp.sum(grads * grads) + jnp.sum(gb2 * gb2))
    factor = jnp.minimum(1.0, clip_limit / (norm + 1e-06))
    grads, gb2 = grads * factor, gb2 * factor
    at = lax.axis_index(AXES) * width
    own = lax.dynamic_slice_in_dim(grads, at, width, axis=1)
    full_one, full_two = grads[:fan_in], grads[fan_in + 1 :].T
    own_one, own_bias, own_two = own[:fan_in], own[fan_in], own[fan_in + 1 :].T
    dot = functools.partial(jnp.dot, precision=highest)
    keep, add = beta_stat, 1.0 - beta_stat
    m1, v1, b1 = adam_step(b_first, own_bias, m_first, v_first)
    m2, v2, b2 = adam_step(b_second, gb2, m_second, v_second)
    return (
        loss, count, norm, own_one, own_two,
        w_first - rate_first * dot(l_first_root, dot(full_one, r_first_root)),
        w_second - rate_second * dot(dot(l_second_root, full_two), r_second_root),
        keep * l_first + add * dot(full_one, full_one.T),
        keep * r_first + add * dot(full_one.T, own_one),
        keep * l_second + add * dot(own_two, full_two.T),
        keep * r_second + add * dot(full_two.T, full_two),
        m1, v1, b1, m2, v2, b2,
    )


def solution(mesh):
    split0 = P(AXES)
    rows = P(AXES, None)
    columns = P(None, AXES)
    whole = P()
    fast = mesh.shape["dp"] == 16 and mesh.shape["shard"] == 2

    def per_device(*args):
        width = args[4].shape[1]
        return (fast_device if fast and 2 * width == LANES else general_device)(*args)

    return jax.shard_map(
        per_device,
        mesh=mesh,
        in_specs=(
            rows, rows, split0, split0, columns, rows, split0, whole, whole, columns, rows, whole,
            whole, columns, rows, whole, split0, split0, whole, whole,
        ),
        out_specs=(
            whole, whole, whole, columns, rows, columns, rows, whole, columns, rows, whole,
            split0, split0, split0, whole, whole, whole,
        ),
        check_vma=False,
    )
```
